256 devices in a mesh: row: 16 (over y, z_hi, core), col: 16 (over x, z_lo).
Axes of the slice: x: 4, y: 4, z: 8 (z_hi: 2, z_lo: 4; z = z_hi * 4 + z_lo), core: 2. Of those that a mesh axis runs over, the one named last changes fastest.
Arguments:
- activations: bfloat16 [2048, 12800], P('row', 'col'), may hold values from -6 to 6
- task_weight: float32 [16], replicated, may hold values from 0.0625 to 0.25
Outputs:
- trailing: float32 [12800, 12800], P('row', 'col')
- panels: float32 [12800, 512], P('row', 'col')
The draws below stay inside these ranges and needn't reach their ends.
All inputs are finite; a program needn't handle non-finite values.
Results may differ from the reference program's by a relative error of at most 0.0042.
Values may be sent and summed in bfloat16 or wider, within the bound.
A program may use at most 64 MiB of HBM per device.

```python
import math
import jax
import jax.numpy as jnp
from jax import lax

NF = 12800
TASKS = 16
TOK = 128
PANEL = 256


def steps_of(own_key, shape, pieces, low, top_value):
    def one(axis_at, blocks):
        heights = jax.random.uniform(jax.random.fold_in(jax.random.fold_in(own_key, 6), axis_at), (blocks,), jnp.float32, low / len(pieces), top_value / len(pieces))
        return jnp.repeat(jnp.exp(heights), shape[axis_at] // blocks).reshape((-1,) + (1,) * (len(shape) - axis_at - 1))

    level = one(*pieces[0])
    for cut in pieces[1:]:
        level = level * one(*cut)
    return level


def centred(stream_key, dims, spread, limit, split=(), kind=jnp.bfloat16):
    entries = jax.random.normal(stream_key, dims, jnp.float32) * spread
    if len(split) > 0:
        entries = steps_of(stream_key, dims, split, -0.22, 0.18) * entries
    return jnp.clip(entries, min=-limit, max=limit).astype(kind)


def setup_inputs(seed: int = 0) -> dict:
    keys = jax.random.split(jax.random.key(seed), 3)
    activations = centred(keys[0], (TASKS * TOK, NF), 1.0, 6.0, ((0, 16), (1, 16)))
    task_weight = jnp.clip(jnp.exp(jax.random.uniform(keys[1], (TASKS,), jnp.float32, math.log(0.0625), math.log(0.25))), 0.0625, 0.25)
    return {"activations": activations, "task_weight": task_weight}


alpha_scale = 0.9
ridge_value = 0.2

def reference(activations, task_weight):
    factor = jnp.repeat(jnp.sqrt(task_weight / TOK), TOK)
    scaled = (activations.astype(jnp.float32) * factor[:, None]).astype(jnp.bfloat16)
    gram_full = jnp.dot(scaled.T.astype(jnp.float32), scaled.astype(jnp.float32), preferred_element_type=jnp.float32)
    indices = jnp.arange(NF)
    on_diagonal = indices[:, None] == indices[None, :]
    matrix = jnp.where(on_diagonal, gram_full + ridge_value, alpha_scale * gram_full)
    panel_list = []
    for panel_index in range(2):
        offset = panel_index * PANEL
        panel_strip = matrix[:, offset:offset + PANEL]
        factor_lower = jnp.linalg.cholesky(panel_strip[offset:offset + PANEL])
        solved = jax.scipy.linalg.solve_triangular(factor_lower, panel_strip.T, lower=True).T
        panel_cols = jnp.concatenate([jnp.zeros((offset, PANEL), jnp.float32), factor_lower, solved[offset + PANEL:]], 0)
        matrix = matrix - jnp.dot(panel_cols, panel_cols.T, precision=lax.Precision.HIGHEST)
        panel_list.append(panel_cols)
    kept_rows = indices >= 2 * PANEL
    trailing = jnp.where(kept_rows[:, None] & kept_rows[None, :], matrix, 0.0)
    return (trailing, jnp.concatenate(panel_list, 1))
```

```python
import jax
import jax.numpy as jnp
from jax import lax
from jax.experimental import pallas as pl
from jax.experimental.pallas import tpu as pltpu
from jax.sharding import PartitionSpec as P

TOK = 128
PANEL = 256
LEAF = 16

alpha_scale = 0.9
ridge_value = 0.2

F32 = jnp.float32
BF = jnp.bfloat16
MESH = pl.DeviceIdType.MESH


def dot_nt(a, b):
    return lax.dot_general(a, b, (((1,), (1,)), ((), ())), preferred_element_type=F32)


def dot_tn(a, b):
    return lax.dot_general(a, b, (((0,), (0,)), ((), ())), preferred_element_type=F32)


def split3(x):
    high = x.astype(BF)
    rest = x - high.astype(F32)
    mid = rest.astype(BF)
    low = (rest - mid.astype(F32)).astype(BF)
    return high, mid, low


def six_left(x):
    h, m, l = split3(x)
    return jnp.concatenate([h, h, h, m, m, l], 0)


def six_right(x):
    h, m, l = split3(x)
    return jnp.concatenate([h, m, l, h, m, h], 0)


def two(x):
    high = x.astype(BF)
    return high, (x - high.astype(F32)).astype(BF)


def sub_cast(x, s):
    return jnp.broadcast_to(x[s : s + 1, :], (8, 128))


def lane_cast(x, k):
    return jnp.broadcast_to(x[:, k : k + 1], (8, 128))


def chain8(s, rows, cols):
    for k in range(8):
        r = lax.rsqrt(s[k, k])
        for j in range(k + 1, 8):
            s[j, k] = s[j, k] * r
        for q in range(k + 1, 8):
            for j in range(q, 8):
                s[j, q] = s[j, q] - s[j, k] * s[q, k]
        rows[k] = rows[k] * r
        for j in range(k + 1, 8):
            rows[j] = rows[j] - s[j, k] * rows[k]
        if cols is not None:
            cols[k] = cols[k] * r
            for q in range(k + 1, 8):
                cols[q] = cols[q] - cols[k] * s[q, k]


def leaf_factor(m4, kb, leaf):
    i0 = kb * 16 + 2 * leaf
    o = LEAF * leaf
    d0 = m4[i0, kb]
    d1 = m4[i0 + 1, kb]
    s = {}
    for k in range(8):
        column = lane_cast(d0, o + k)
        for j in range(k, 8):
            s[j, k] = sub_cast(column, j)
    cols = [lane_cast(d1, o + k) for k in range(16)]
    upper = [m4[i0, :, q, :] for q in range(8)]
    first = cols[:8]
    chain8(s, upper, first)
    for q in range(8):
        m4[i0, :, q, :] = upper[q]
    lower = [m4[i0 + 1, :, q, :] for q in range(8)]
    second = cols[8:]
    for k in range(8):
        t = [sub_cast(first[k], q) for q in range(8)]
        for q in range(8):
            second[q] = second[q] - first[k] * t[q]
        for q in range(8):
            lower[q] = lower[q] - t[q] * upper[k]
    s = {}
    for k in range(8):
        for j in range(k, 8):
            s[j, k] = sub_cast(second[k], j)
    chain8(s, lower, None)
    for q in range(8):
        m4[i0 + 1, :, q, :] = lower[q]


def inner_update(m4, kb, leaf):
    i0 = kb * 16 + 2 * leaf
    u = m4[pl.ds(i0, 2), pl.ds(kb, 5)]
    tiles = [u[:, t].reshape(16, 128) for t in range(5)]
    left = six_left(tiles[0])[:, LEAF * (leaf + 1) :]
    up = dot_tn(left, six_right(jnp.concatenate(tiles, 1)))
    for q in range((7 - leaf) * 2):
        for t in range(5):
            m4[i0 + 2 + q, kb + t] = (
                m4[i0 + 2 + q, kb + t] - up[8 * q : 8 * q + 8, 128 * t : 128 * t + 128]
            )


def rest_update(m4, kb, b):
    left = six_left(m4[pl.ds(kb * 16, 16), b].reshape(128, 128))
    for half in range(2):
        w = jnp.concatenate(
            [m4[pl.ds(kb * 16, 16), kb + 1 + 2 * half + t].reshape(128, 128) for t in range(2)], 1
        )
        up = dot_tn(left, six_right(w))
        for t in range(2):
            tt = kb + 1 + 2 * half + t
            m4[pl.ds(b * 16, 16), tt] = m4[pl.ds(b * 16, 16), tt] - up[
                :, 128 * t : 128 * t + 128
            ].reshape(16, 8, 128)


def factor(m4):
    def block(kb, _):
        for leaf in range(8):
            leaf_factor(m4, kb, leaf)
            if leaf < 7:
                inner_update(m4, kb, leaf)

        def rest(b, _):
            rest_update(m4, kb, b)
            return 0

        lax.fori_loop(kb + 1, 4, rest, 0)
        return 0

    lax.fori_loop(0, 4, block, 0)


def gather_kernel(act, weight, cs, rs, ss, send, crecv, rrecv, srecv):
    r = lax.axis_index("row")
    c = lax.axis_index("col")
    y, h, k = r // 4, (r // 2) % 2, r % 2
    x, l = c // 4, c % 4

    def row_at(yy, hh, kk):
        return 4 * ((yy + 4) % 4) + 2 * hh + kk

    def col_at(xx, ll):
        return 4 * ((xx + 4) % 4) + ll

    zring = [(r, col_at(x, (l + d) % 4)) for d in (1, 2, 3)]
    zring += [(row_at(y, 1 - h, k), col_at(x, (l + d) % 4)) for d in (0, 1, 2, 3)]
    partners = zring + [
        (r, col_at(x + 1, l)),
        (r, col_at(x - 1, l)),
        (row_at(y + 1, h, k), c),
        (row_at(y - 1, h, k), c),
        (row_at(y, h, 1 - k), c),
    ]
    barrier = pltpu.get_barrier_semaphore()
    for p in partners:
        pl.semaphore_signal(barrier, inc=1, device_id=p, device_id_type=MESH)

    @pl.when(r != c)
    def _():
        pl.semaphore_signal(barrier, inc=1, device_id=(c, r), device_id_type=MESH)

    value = jnp.full((8, 128), weight[r], F32)
    scale = jnp.sqrt(value / TOK)[0:1, 0:1]
    for f in range(0, 800, 128):
        n = min(128, 800 - f)
        part = (act[:, f : f + n].astype(F32) * scale).astype(BF).astype(F32)
        cs[r, f : f + n, :] = part.T.astype(BF)

    pl.semaphore_wait(barrier, jnp.where(r == c, len(partners), len(partners) + 1))

    pending = []
    count = [0]

    def copy(src, dst, recv, target, cond=None):
        d = pltpu.make_async_remote_copy(
            src_ref=src,
            dst_ref=dst,
            send_sem=send.at[count[0]],
            recv_sem=recv,
            device_id=target,
            device_id_type=MESH,
        )
        count[0] += 1
        if cond is None:
            d.start()
        else:
            pl.when(cond)(d.start)
        pending.append((cond, d))

    def send_c(t, target):
        copy(cs.at[t], cs.at[t], crecv.at[t], target)

    def send_r(t, target):
        copy(rs.at[t], rs.at[t], rrecv.at[t], target)

    def s_ref(t, half):
        return ss.at[t, pl.ds(256 * half, 256)]

    def send_s(t, half, target, cond=None):
        copy(s_ref(t, half), s_ref(t, half), srecv.at[t, half], target, cond)

    def arrived(ref, sem):
        pltpu.make_async_remote_copy(
            src_ref=ref, dst_ref=ref, send_sem=send.at[0], recv_sem=sem, device_id=(r, c), device_id_type=MESH
        ).wait_recv()

    def wait_c(t):
        arrived(cs.at[t], crecv.at[t])

    def wait_r(t):
        arrived(rs.at[t], rrecv.at[t])

    def wait_s(t, half):
        arrived(s_ref(t, half), srecv.at[t, half])

    twin = row_at(y, 1 - h, k)
    up, down = row_at(y + 1, h, k), row_at(y - 1, h, k)
    right, left = col_at(x + 1, l), col_at(x - 1, l)
    other = row_at(y, h, 1 - k)

    @pl.when(c == 0)
    def _():
        ss[r] = cs[r, 0:512]

    at_l0 = l == 0
    source = c == 0
    side = jnp.logical_and(at_l0, x % 2 == 1)
    for half in range(2):
        send_s(r, half, (r, 4), source)
        send_s(r, half, (r, 12), source)

    @pl.when(r == c)
    def _():
        rs[c] = cs[r]

    copy(cs.at[r], rs.at[r], rrecv.at[r], (c, r), r != c)
    send_c(r, (twin, c))
    send_c(r, (up, c))
    send_c(r, (down, c))

    for half in range(2):

        @pl.when(jnp.logical_and(at_l0, x != 0))
        def _():
            wait_s(r, half)

        send_s(r, half, (r, 8), jnp.logical_and(at_l0, x == 1 + 2 * half))
        for p in zring:
            send_s(r, half, p, at_l0)

    for half in range(2):

        @pl.when(l != 0)
        def _():
            wait_s(r, half)

        wait_s(twin, half)
        for t in (r, twin):
            send_s(t, half, (up, c))
            send_s(t, half, (down, c))
            send_s(t, half, (other, c))

    for half in range(2):
        for hh in range(2):
            wait_s(row_at(y - 1, hh, k), half)
            wait_s(row_at(y + 1, hh, k), half)
        send_s(row_at(y - 1, 0, k), half, (up, c))
        send_s(row_at(y + 1, 1, k), half, (down, c))
        for hh in range(2):
            send_s(row_at(y - 1, hh, k), half, (other, c))
            send_s(row_at(y + 1, hh, k), half, (other, c))

    @pl.when(r != c)
    def _():
        wait_r(c)

    for d in (1, 2, 3):
        send_r(c, (r, col_at(x, (l + d) % 4)))
    send_r(c, (r, right))
    send_r(c, (r, left))

    wait_c(twin)
    send_c(twin, (up, c))
    send_c(twin, (down, c))
    send_c(r, (other, c))
    send_c(twin, (other, c))

    for half in range(2):
        for hh in range(2):
            wait_s(row_at(y + 2, hh, k), half)
            send_s(row_at(y + 2, hh, k), half, (other, c))

    for d in (1, 2, 3):
        t = col_at(x, (l + d) % 4)
        wait_r(t)
        send_r(t, (r, right))
        send_r(t, (r, left))

    for hh in range(2):
        wait_c(row_at(y - 1, hh, k))
        wait_c(row_at(y + 1, hh, k))
    send_c(row_at(y - 1, 0, k), (up, c))
    send_c(row_at(y + 1, 1, k), (down, c))
    for hh in range(2):
        send_c(row_at(y - 1, hh, k), (other, c))
        send_c(row_at(y + 1, hh, k), (other, c))

    for d in range(4):
        ll = (l + d) % 4
        wait_r(col_at(x - 1, ll))
        wait_r(col_at(x + 1, ll))
        if d < 2:
            send_r(col_at(x - 1, ll), (r, right))
        else:
            send_r(col_at(x + 1, ll), (r, left))

    for hh in range(2):
        wait_c(row_at(y + 2, hh, k))
        send_c(row_at(y + 2, hh, k), (other, c))
    for ll in range(4):
        wait_r(col_at(x + 2, ll))
    for d in range(4):
        for hh in range(2):
            wait_c(row_at(y + d, hh, 1 - k))
            for half in range(2):
                wait_s(row_at(y + d, hh, 1 - k), half)

    for cond, d in pending:
        if cond is None:
            d.wait_send()
        else:
            pl.when(cond)(d.wait_send)


def compute_kernel(cs, rs, ss, trailing, panels, m4, yr, yc, pr, pc):
    r = lax.axis_index("row")
    c = lax.axis_index("col")
    s_all = jnp.concatenate([ss[t] for t in range(16)], 1)
    for n in range(2):
        g = dot_nt(s_all, s_all[256 * n : 256 * n + 256])
        i = lax.broadcasted_iota(jnp.int32, (512, 256), 0)
        j = lax.broadcasted_iota(jnp.int32, (512, 256), 1) + 256 * n
        g = jnp.where(i == j, g + ridge_value, alpha_scale * g)
        for t in range(2):
            m4[:, 2 * n + t] = g[:, 128 * t : 128 * t + 128].reshape(64, 8, 128)
            m4[:, 4 + 2 * n + t] = jnp.where(i == j, 1.0, 0.0)[:, 128 * t : 128 * t + 128].reshape(64, 8, 128)
    factor(m4)

    c_all = jnp.concatenate([cs[t] for t in range(16)], 1)
    r_all = jnp.concatenate([rs[t] for t in range(16)], 1)
    for n in range(2):
        yr[:, 256 * n : 256 * n + 256] = alpha_scale * dot_nt(r_all, s_all[256 * n : 256 * n + 256])
        yc[:, 256 * n : 256 * n + 256] = alpha_scale * dot_nt(c_all, s_all[256 * n : 256 * n + 256])

    wide = [jnp.concatenate([m4[pl.ds(16 * b, 16), 4 + t].reshape(128, 128) for b in range(4)], 0) for t in range(4)]
    w_high, w_low = two(jnp.concatenate(wide, 1))
    for y_ref, p_ref in ((yr, pr), (yc, pc)):
        y_high, y_low = two(y_ref[...])
        p = dot_nt(
            jnp.concatenate([y_high, y_high, y_low], 1), jnp.concatenate([w_high, w_low, w_high], 1)
        )
        p_ref[...] = p

    w_mine = jnp.concatenate([m4[pl.ds(4 * c, 4), 4 + t].reshape(32, 128) for t in range(4)], 1)
    wm_high, wm_low = two(w_mine)
    y_high, y_low = two(yr[...])
    mine = dot_nt(
        jnp.concatenate([y_high, y_high, y_low], 1), jnp.concatenate([wm_high, wm_low, wm_high], 1)
    )
    panels[...] = mine
    u_row = lax.broadcasted_iota(jnp.int32, (128, 128), 0) + 32 * c

    @pl.when(r == 0)
    def _():
        for t in range(4):
            u = m4[pl.ds(4 * c, 4), t].reshape(32, 128)
            u = jnp.concatenate([u, u, u, u], 0)
            j = lax.broadcasted_iota(jnp.int32, (128, 128), 1) + 128 * t
            u = jnp.where(j >= u_row, u, 0.0)
            panels[128 * t : 128 * t + 128, :] = u.T[:, 0:32]

    pr_high, pr_low = two(pr[...])
    pc_high, pc_low = two(pc[...])
    p_left = jnp.concatenate([pr_high, pr_high, pr_low], 1)
    p_right = jnp.concatenate([pc_high, pc_low, pc_high], 1)
    row0 = jnp.where(r == 0, 512, 0)
    col0 = jnp.where(c == 0, 512, 0)
    for n in range(0, 800, 256):
        w = min(256, 800 - n)
        g = dot_nt(r_all, c_all[n : n + w])
        pp = dot_nt(p_left, p_right[n : n + w])
        i = lax.broadcasted_iota(jnp.int32, (800, w), 0)
        j = lax.broadcasted_iota(jnp.int32, (800, w), 1) + n
        m = jnp.where(i == jnp.where(r == c, j, -1), g + ridge_value, alpha_scale * g) - pp
        trailing[:, n : n + w] = jnp.where(jnp.logical_and(i >= row0, j >= col0), m, 0.0)


def body(activations, task_weight):
    vmem = pl.BlockSpec(memory_space=pltpu.VMEM)
    slab = jax.ShapeDtypeStruct((16, 800, 128), BF)
    first = jax.ShapeDtypeStruct((16, 512, 128), BF)
    cs, rs, ss = pl.pallas_call(
        gather_kernel,
        out_shape=(slab, slab, first),
        in_specs=[vmem, pl.BlockSpec(memory_space=pltpu.SMEM)],
        out_specs=(vmem, vmem, vmem),
        scratch_shapes=[
            pltpu.SemaphoreType.DMA((128,)),
            pltpu.SemaphoreType.DMA((16,)),
            pltpu.SemaphoreType.DMA((16,)),
            pltpu.SemaphoreType.DMA((16, 2)),
        ],
        compiler_params=pltpu.CompilerParams(
            collective_id=0, has_side_effects=True, vmem_limit_bytes=60 << 20
        ),
    )(activations, task_weight)
    return pl.pallas_call(
        compute_kernel,
        out_shape=(
            jax.ShapeDtypeStruct((800, 800), F32),
            jax.ShapeDtypeStruct((800, 32), F32),
        ),
        in_specs=[vmem] * 3,
        out_specs=(vmem, vmem),
        scratch_shapes=[
            pltpu.VMEM((64, 8, 8, 128), F32),
            pltpu.VMEM((800, 512), F32),
            pltpu.VMEM((800, 512), F32),
            pltpu.VMEM((800, 512), F32),
            pltpu.VMEM((800, 512), F32),
        ],
        compiler_params=pltpu.CompilerParams(vmem_limit_bytes=60 << 20),
    )(cs, rs, ss)


def solution(mesh):
    placed = (P("row", "col"), P())
    return jax.shard_map(
        body,
        mesh=mesh,
        in_specs=placed,
        out_specs=(P("row", "col"), P("row", "col")),
        check_vma=False,
    )
```

```python
import jax
import jax.numpy as jnp
from jax import lax
from jax.experimental import pallas as pl
from jax.experimental.pallas import tpu as pltpu
from jax.sharding import PartitionSpec as P

TOK = 128
PANEL = 256
LEAF = 16

alpha_scale = 0.9
ridge_value = 0.2

F32 = jnp.float32
BF = jnp.bfloat16
MESH = pl.DeviceIdType.MESH


def dot_nt(a, b):
    return lax.dot_general(a, b, (((1,), (1,)), ((), ())), preferred_element_type=F32)


def dot_tn(a, b):
    return lax.dot_general(a, b, (((0,), (0,)), ((), ())), preferred_element_type=F32)


def split3(x):
    high = x.astype(BF)
    rest = x - high.astype(F32)
    mid = rest.astype(BF)
    low = (rest - mid.astype(F32)).astype(BF)
    return high, mid, low


def six_left(x):
    h, m, l = split3(x)
    return jnp.concatenate([h, h, h, m, m, l], 0)


def six_right(x):
    h, m, l = split3(x)
    return jnp.concatenate([h, m, l, h, m, h], 0)


def two(x):
    high = x.astype(BF)
    return high, (x - high.astype(F32)).astype(BF)


def sub_cast(x, s):
    return jnp.broadcast_to(x[s : s + 1, :], (8, 128))


def lane_cast(x, k):
    return jnp.broadcast_to(x[:, k : k + 1], (8, 128))


def chain8(s, rows, cols):
    for k in range(8):
        r = lax.rsqrt(s[k, k])
        for j in range(k + 1, 8):
            s[j, k] = s[j, k] * r
        for q in range(k + 1, 8):
            for j in range(q, 8):
                s[j, q] = s[j, q] - s[j, k] * s[q, k]
        rows[k] = rows[k] * r
        for j in range(k + 1, 8):
            rows[j] = rows[j] - s[j, k] * rows[k]
        if cols is not None:
            cols[k] = cols[k] * r
            for q in range(k + 1, 8):
                cols[q] = cols[q] - cols[k] * s[q, k]


def leaf_factor(m4, kb, leaf):
    i0 = kb * 16 + 2 * leaf
    o = LEAF * leaf
    d0 = m4[i0, kb]
    d1 = m4[i0 + 1, kb]
    s = {}
    for k in range(8):
        column = lane_cast(d0, o + k)
        for j in range(k, 8):
            s[j, k] = sub_cast(column, j)
    cols = [lane_cast(d1, o + k) for k in range(16)]
    upper = [m4[i0, :, q, :] for q in range(8)]
    first = cols[:8]
    chain8(s, upper, first)
    for q in range(8):
        m4[i0, :, q, :] = upper[q]
    lower = [m4[i0 + 1, :, q, :] for q in range(8)]
    second = cols[8:]
    for k in range(8):
        t = [sub_cast(first[k], q) for q in range(8)]
        for q in range(8):
            second[q] = second[q] - first[k] * t[q]
        for q in range(8):
            lower[q] = lower[q] - t[q] * upper[k]
    s = {}
    for k in range(8):
        for j in range(k, 8):
            s[j, k] = sub_cast(second[k], j)
    chain8(s, lower, None)
    for q in range(8):
        m4[i0 + 1, :, q, :] = lower[q]


def inner_update(m4, kb, leaf):
    i0 = kb * 16 + 2 * leaf
    u = m4[pl.ds(i0, 2), pl.ds(kb, 5)]
    tiles = [u[:, t].reshape(16, 128) for t in range(5)]
    left = six_left(tiles[0])[:, LEAF * (leaf + 1) :]
    up = dot_tn(left, six_right(jnp.concatenate(tiles, 1)))
    for q in range((7 - leaf) * 2):
        for t in range(5):
            m4[i0 + 2 + q, kb + t] = (
                m4[i0 + 2 + q, kb + t] - up[8 * q : 8 * q + 8, 128 * t : 128 * t + 128]
            )


def rest_update(m4, kb, b):
    left = six_left(m4[pl.ds(kb * 16, 16), b].reshape(128, 128))
    for half in range(2):
        w = jnp.concatenate(
            [m4[pl.ds(kb * 16, 16), kb + 1 + 2 * half + t].reshape(128, 128) for t in range(2)], 1
        )
        up = dot_tn(left, six_right(w))
        for t in range(2):
            tt = kb + 1 + 2 * half + t
            m4[pl.ds(b * 16, 16), tt] = m4[pl.ds(b * 16, 16), tt] - up[
                :, 128 * t : 128 * t + 128
            ].reshape(16, 8, 128)


def factor(m4, hooks):
    def block(kb, _):
        for leaf in range(8):
            for at, run in hooks:
                if at % 8 == leaf:
                    pl.when(kb == at // 8)(run)
            leaf_factor(m4, kb, leaf)
            if leaf < 7:
                inner_update(m4, kb, leaf)

        def rest(b, _):
            rest_update(m4, kb, b)
            return 0

        lax.fori_loop(kb + 1, 4, rest, 0)
        return 0

    lax.fori_loop(0, 4, block, 0)


def kernel(act, weight, trailing, panels, cs, rs, ss, m4, yr, yc, pr, pc, send, crecv, rrecv, srecv):
    r = lax.axis_index("row")
    c = lax.axis_index("col")
    y, h, k = r // 4, (r // 2) % 2, r % 2
    x, l = c // 4, c % 4

    def row_at(yy, hh, kk):
        return 4 * ((yy + 4) % 4) + 2 * hh + kk

    def col_at(xx, ll):
        return 4 * ((xx + 4) % 4) + ll

    zring = [(r, col_at(x, (l + d) % 4)) for d in (1, 2, 3)]
    zring += [(row_at(y, 1 - h, k), col_at(x, (l + d) % 4)) for d in (0, 1, 2, 3)]
    partners = zring + [
        (r, col_at(x + 1, l)),
        (r, col_at(x - 1, l)),
        (row_at(y + 1, h, k), c),
        (row_at(y - 1, h, k), c),
        (row_at(y, h, 1 - k), c),
    ]
    barrier = pltpu.get_barrier_semaphore()
    for p in partners:
        pl.semaphore_signal(barrier, inc=1, device_id=p, device_id_type=MESH)

    @pl.when(r != c)
    def _():
        pl.semaphore_signal(barrier, inc=1, device_id=(c, r), device_id_type=MESH)

    scale = jnp.sqrt(jnp.full((8, 128), weight[r], F32) / TOK)[0:1, 0:1]
    cs[r] = (act[...].astype(F32) * scale).astype(BF)

    @pl.when(c == 0)
    def _():
        ss[r] = cs[r, 0:512]

    @pl.when(r == c)
    def _():
        rs[c] = cs[r]

    pl.semaphore_wait(barrier, jnp.where(r == c, len(partners), len(partners) + 1))

    pending = []

    def copy(src, dst, recv, target, cond=None):
        d = pltpu.make_async_remote_copy(
            src_ref=src,
            dst_ref=dst,
            send_sem=send.at[len(pending)],
            recv_sem=recv,
            device_id=target,
            device_id_type=MESH,
        )
        if cond is None:
            d.start()
        else:
            pl.when(cond)(d.start)
        pending.append((cond, src))

    def send_c(t, target):
        copy(cs.at[t], cs.at[t], crecv.at[t], target)

    def send_r(t, target):
        copy(rs.at[t], rs.at[t], rrecv.at[t], target)

    def s_ref(t, half):
        return ss.at[t, pl.ds(256 * half, 256)]

    def send_s(t, half, target, cond=None):
        copy(s_ref(t, half), s_ref(t, half), srecv.at[t, half], target, cond)

    def arrived(ref, sem):
        pltpu.make_async_remote_copy(
            src_ref=ref, dst_ref=ref, send_sem=send.at[0], recv_sem=sem, device_id=(r, c), device_id_type=MESH
        ).wait_recv()

    def wait_c(t):
        arrived(cs.at[t], crecv.at[t])

    def wait_r(t):
        arrived(rs.at[t], rrecv.at[t])

    def wait_s(t, half):
        arrived(s_ref(t, half), srecv.at[t, half])

    twin = row_at(y, 1 - h, k)
    up, down = row_at(y + 1, h, k), row_at(y - 1, h, k)
    right, left = col_at(x + 1, l), col_at(x - 1, l)
    other = row_at(y, h, 1 - k)

    at_l0 = l == 0
    source = c == 0
    for half in range(2):
        send_s(r, half, (r, 4), source)
        send_s(r, half, (r, 12), source)
    copy(cs.at[r], rs.at[r], rrecv.at[r], (c, r), r != c)

    for half in range(2):

        @pl.when(jnp.logical_and(at_l0, x != 0))
        def _():
            wait_s(r, half)

        send_s(r, half, (r, 8), jnp.logical_and(at_l0, x == 1 + 2 * half))
        for p in zring:
            send_s(r, half, p, at_l0)

    for half in range(2):

        @pl.when(l != 0)
        def _():
            wait_s(r, half)

        wait_s(twin, half)
        for t in (r, twin):
            send_s(t, half, (up, c))
            send_s(t, half, (down, c))
            send_s(t, half, (other, c))

    @pl.when(r != c)
    def _():
        wait_r(c)

    for d in (1, 2, 3):
        send_r(c, (r, col_at(x, (l + d) % 4)))
    send_r(c, (r, right))
    send_r(c, (r, left))

    for half in range(2):
        for hh in range(2):
            wait_s(row_at(y - 1, hh, k), half)
            wait_s(row_at(y + 1, hh, k), half)
        send_s(row_at(y - 1, 0, k), half, (up, c))
        send_s(row_at(y + 1, 1, k), half, (down, c))
        for hh in range(2):
            send_s(row_at(y - 1, hh, k), half, (other, c))
            send_s(row_at(y + 1, hh, k), half, (other, c))

    send_c(r, (twin, c))
    send_c(r, (up, c))
    send_c(r, (down, c))
    send_c(r, (other, c))

    for half in range(2):
        for hh in range(2):
            wait_s(row_at(y + 2, hh, k), half)
            send_s(row_at(y + 2, hh, k), half, (other, c))
    for d in range(4):
        for hh in range(2):
            for half in range(2):
                wait_s(row_at(y + d, hh, 1 - k), half)

    near = [col_at(x, (l + d) % 4) for d in range(4)]
    on_left = [col_at(x - 1, (l + d) % 4) for d in range(4)]
    on_right = [col_at(x + 1, (l + d) % 4) for d in range(4)]
    below = [row_at(y - 1, hh, k) for hh in range(2)]
    above = [row_at(y + 1, hh, k) for hh in range(2)]
    beyond = [row_at(y + 2, hh, k) for hh in range(2)]

    def line(d):
        t = near[d]
        wait_r(t)
        send_r(t, (r, right))
        send_r(t, (r, left))

    def ring(d):
        wait_r(on_left[d])
        wait_r(on_right[d])
        if d < 2:
            send_r(on_left[d], (r, right))
        else:
            send_r(on_right[d], (r, left))

    def twins():
        wait_c(twin)
        send_c(twin, (up, c))
        send_c(twin, (down, c))
        send_c(twin, (other, c))

    def ends():
        for hh in range(2):
            wait_c(below[hh])
            wait_c(above[hh])
        send_c(below[0], (up, c))
        send_c(above[1], (down, c))
        for hh in range(2):
            send_c(below[hh], (other, c))
            send_c(above[hh], (other, c))

    def far():
        for hh in range(2):
            wait_c(beyond[hh])
            send_c(beyond[hh], (other, c))

    hooks = [
        (3, lambda: line(1)),
        (6, lambda: line(2)),
        (8, lambda: ring(0)),
        (10, twins),
        (11, lambda: line(3)),
        (14, lambda: ring(1)),
        (17, ends),
        (20, lambda: ring(2)),
        (23, lambda: ring(3)),
        (25, far),
    ]

    s_all = jnp.concatenate([ss[t] for t in range(16)], 1)
    for n in range(2):
        g = dot_nt(s_all, s_all[256 * n : 256 * n + 256])
        i = lax.broadcasted_iota(jnp.int32, (512, 256), 0)
        j = lax.broadcasted_iota(jnp.int32, (512, 256), 1) + 256 * n
        g = jnp.where(i == j, g + ridge_value, alpha_scale * g)
        one = jnp.where(i == j, 1.0, 0.0)
        for t in range(2):
            m4[:, 2 * n + t] = g[:, 128 * t : 128 * t + 128].reshape(64, 8, 128)
            m4[:, 4 + 2 * n + t] = one[:, 128 * t : 128 * t + 128].reshape(64, 8, 128)
    factor(m4, hooks)

    for d in range(4):
        for hh in range(2):
            wait_c(row_at(y + d, hh, 1 - k))
    s_again = jnp.concatenate([ss[t] for t in range(16)], 1)
    c_all = jnp.concatenate([cs[t] for t in range(16)], 1)
    for n in range(2):
        yc[:, 256 * n : 256 * n + 256] = alpha_scale * dot_nt(c_all, s_again[256 * n : 256 * n + 256])

    wide = [jnp.concatenate([m4[pl.ds(16 * b, 16), 4 + t].reshape(128, 128) for b in range(4)], 0) for t in range(4)]
    w_high, w_low = two(jnp.concatenate(wide, 1))
    w_right = jnp.concatenate([w_high, w_low, w_high], 1)

    def solve(y_ref, p_ref):
        y_high, y_low = two(y_ref[...])
        p_ref[...] = dot_nt(jnp.concatenate([y_high, y_high, y_low], 1), w_right)

    solve(yc, pc)

    for ll in range(4):
        wait_r(col_at(x + 2, ll))
    r_all = jnp.concatenate([rs[t] for t in range(16)], 1)
    for n in range(2):
        yr[:, 256 * n : 256 * n + 256] = alpha_scale * dot_nt(r_all, s_again[256 * n : 256 * n + 256])
    solve(yr, pr)

    w_mine = jnp.concatenate([m4[pl.ds(4 * c, 4), 4 + t].reshape(32, 128) for t in range(4)], 1)
    wm_high, wm_low = two(w_mine)
    y_high, y_low = two(yr[...])
    panels[...] = dot_nt(
        jnp.concatenate([wm_high, wm_low, wm_high], 1), jnp.concatenate([y_high, y_high, y_low], 1)
    )

    @pl.when(r == 0)
    def _():
        i = lax.broadcasted_iota(jnp.int32, (32, 128), 0) + 32 * c
        for t in range(4):
            u = m4[pl.ds(4 * c, 4), t].reshape(32, 128)
            j = lax.broadcasted_iota(jnp.int32, (32, 128), 1) + 128 * t
            panels[:, 128 * t : 128 * t + 128] = jnp.where(j >= i, u, 0.0)

    pr_high, pr_low = two(pr[...])
    pc_high, pc_low = two(pc[...])
    p_left = jnp.concatenate([pr_high, pr_high, pr_low], 1)
    p_right = jnp.concatenate([pc_high, pc_low, pc_high], 1)
    row0 = jnp.where(r == 0, 512, 0)
    col0 = jnp.where(c == 0, 512, 0)
    for n in range(0, 800, 256):
        w = min(256, 800 - n)
        g = dot_nt(r_all, c_all[n : n + w])
        pp = dot_nt(p_left, p_right[n : n + w])
        i = lax.broadcasted_iota(jnp.int32, (800, w), 0)
        j = lax.broadcasted_iota(jnp.int32, (800, w), 1) + n
        m = jnp.where(i == jnp.where(r == c, j, -1), g + ridge_value, alpha_scale * g) - pp
        trailing[:, n : n + w] = jnp.where(jnp.logical_and(i >= row0, j >= col0), m, 0.0)

    for at, (cond, src) in enumerate(pending):
        sent = pltpu.make_async_remote_copy(
            src_ref=src, dst_ref=src, send_sem=send.at[at], recv_sem=crecv.at[0], device_id=(other, c), device_id_type=MESH
        ).wait_send
        if cond is None:
            sent()
        else:
            pl.when(cond)(sent)


def body(activations, task_weight):
    vmem = pl.BlockSpec(memory_space=pltpu.VMEM)
    trailing, panels = pl.pallas_call(
        kernel,
        out_shape=(
            jax.ShapeDtypeStruct((800, 800), F32),
            jax.ShapeDtypeStruct((32, 800), F32),
        ),
        in_specs=[vmem, pl.BlockSpec(memory_space=pltpu.SMEM)],
        out_specs=(vmem, vmem),
        scratch_shapes=[
            pltpu.VMEM((16, 800, 128), BF),
            pltpu.VMEM((16, 800, 128), BF),
            pltpu.VMEM((16, 512, 128), BF),
            pltpu.VMEM((64, 8, 8, 128), F32),
            pltpu.VMEM((800, 512), F32),
            pltpu.VMEM((800, 512), F32),
            pltpu.VMEM((800, 512), F32),
            pltpu.VMEM((800, 512), F32),
            pltpu.SemaphoreType.DMA((96,)),
            pltpu.SemaphoreType.DMA((16,)),
            pltpu.SemaphoreType.DMA((16,)),
            pltpu.SemaphoreType.DMA((16, 2)),
        ],
        compiler_params=pltpu.CompilerParams(
            collective_id=0, has_side_effects=True, vmem_limit_bytes=60 << 20
        ),
    )(activations.T, task_weight)
    return trailing, panels.T


def solution(mesh):
    placed = (P("row", "col"), P())
    return jax.shard_map(
        body,
        mesh=mesh,
        in_specs=placed,
        out_specs=(P("row", "col"), P("row", "col")),
        check_vma=False,
    )
```

```python
import jax
import jax.numpy as jnp
from jax import lax
from jax.experimental import pallas as pl
from jax.experimental.pallas import tpu as pltpu
from jax.sharding import PartitionSpec as P

TOK = 128
PANEL = 256
LEAF = 16
PIECES = ((0, 128), (128, 128), (256, 256))

alpha_scale = 0.9
ridge_value = 0.2

F32 = jnp.float32
BF = jnp.bfloat16
MESH = pl.DeviceIdType.MESH


def dot_nt(a, b):
    return lax.dot_general(a, b, (((1,), (1,)), ((), ())), preferred_element_type=F32)


def dot_tn(a, b):
    return lax.dot_general(a, b, (((0,), (0,)), ((), ())), preferred_element_type=F32)


def split3(x):
    high = x.astype(BF)
    rest = x - high.astype(F32)
    mid = rest.astype(BF)
    low = (rest - mid.astype(F32)).astype(BF)
    return high, mid, low


def six_left(x):
    h, m, l = split3(x)
    return jnp.concatenate([h, h, h, m, m, l], 0)


def six_right(x):
    h, m, l = split3(x)
    return jnp.concatenate([h, m, l, h, m, h], 0)


def two(x):
    high = x.astype(BF)
    return high, (x - high.astype(F32)).astype(BF)


def sub_cast(x, s):
    return jnp.broadcast_to(x[s : s + 1, :], (8, 128))


def lane_cast(x, k):
    return jnp.broadcast_to(x[:, k : k + 1], (8, 128))


def chain8(s, rows, cols):
    for k in range(8):
        r = lax.rsqrt(s[k, k])
        for j in range(k + 1, 8):
            s[j, k] = s[j, k] * r
        for q in range(k + 1, 8):
            for j in range(q, 8):
                s[j, q] = s[j, q] - s[j, k] * s[q, k]
        rows[k] = rows[k] * r
        for j in range(k + 1, 8):
            rows[j] = rows[j] - s[j, k] * rows[k]
        if cols is not None:
            cols[k] = cols[k] * r
            for q in range(k + 1, 8):
                cols[q] = cols[q] - cols[k] * s[q, k]


def leaf_factor(m4, kb, leaf):
    i0 = kb * 16 + 2 * leaf
    o = LEAF * leaf
    d0 = m4[i0, kb]
    d1 = m4[i0 + 1, kb]
    s = {}
    for k in range(8):
        column = lane_cast(d0, o + k)
        for j in range(k, 8):
            s[j, k] = sub_cast(column, j)
    cols = [lane_cast(d1, o + k) for k in range(16)]
    upper = [m4[i0, :, q, :] for q in range(8)]
    first = cols[:8]
    chain8(s, upper, first)
    for q in range(8):
        m4[i0, :, q, :] = upper[q]
    lower = [m4[i0 + 1, :, q, :] for q in range(8)]
    second = cols[8:]
    for k in range(8):
        t = [sub_cast(first[k], q) for q in range(8)]
        for q in range(8):
            second[q] = second[q] - first[k] * t[q]
        for q in range(8):
            lower[q] = lower[q] - t[q] * upper[k]
    s = {}
    for k in range(8):
        for j in range(k, 8):
            s[j, k] = sub_cast(second[k], j)
    chain8(s, lower, None)
    for q in range(8):
        m4[i0 + 1, :, q, :] = lower[q]


def inner_update(m4, kb, leaf):
    i0 = kb * 16 + 2 * leaf
    u = m4[pl.ds(i0, 2), pl.ds(kb, 5)]
    tiles = [u[:, t].reshape(16, 128) for t in range(5)]
    left = six_left(tiles[0])[:, LEAF * (leaf + 1) :]
    up = dot_tn(left, six_right(jnp.concatenate(tiles, 1)))
    for q in range((7 - leaf) * 2):
        for t in range(5):
            m4[i0 + 2 + q, kb + t] = (
                m4[i0 + 2 + q, kb + t] - up[8 * q : 8 * q + 8, 128 * t : 128 * t + 128]
            )


def rest_update(m4, kb, b):
    left = six_left(m4[pl.ds(kb * 16, 16), b].reshape(128, 128))
    for half in range(2):
        w = jnp.concatenate(
            [m4[pl.ds(kb * 16, 16), kb + 1 + 2 * half + t].reshape(128, 128) for t in range(2)], 1
        )
        up = dot_tn(left, six_right(w))
        for t in range(2):
            tt = kb + 1 + 2 * half + t
            m4[pl.ds(b * 16, 16), tt] = m4[pl.ds(b * 16, 16), tt] - up[
                :, 128 * t : 128 * t + 128
            ].reshape(16, 8, 128)


def factor(m4, hooks):
    def block(kb, _):
        for leaf in range(8):
            for at, run in hooks:
                if at % 8 == leaf:
                    pl.when(kb == at // 8)(run)
            leaf_factor(m4, kb, leaf)
            if leaf < 7:
                inner_update(m4, kb, leaf)

        def rest(b, _):
            rest_update(m4, kb, b)
            return 0

        lax.fori_loop(kb + 1, jnp.where(kb < 2, kb + 1, 4), rest, 0)
        return 0

    lax.fori_loop(0, 4, block, 0)


def kernel(act, weight, trailing, panels, cs, rs, ss, m4, yr, yc, pr, pc, send, crecv, rrecv, srecv):
    r = lax.axis_index("row")
    c = lax.axis_index("col")
    y, h, k = r // 4, (r // 2) % 2, r % 2
    x, l = c // 4, c % 4

    def row_at(yy, hh, kk):
        return 4 * ((yy + 4) % 4) + 2 * hh + kk

    def col_at(xx, ll):
        return 4 * ((xx + 8) % 4) + ll

    def slot_at(xx, ll):
        return 4 * ((2 * y - xx + 8) % 4) + 2 * ((ll // 2 + k + h) % 2) + ll % 2

    mine = slot_at(x, l)
    goes_row = c
    goes_col = col_at(2 * x - y, 2 * ((h + l // 2 + l % 2) % 2) + k)
    moves = jnp.logical_or(goes_row != r, goes_col != c)
    stays = jnp.logical_not(moves)

    zring = [(r, col_at(x, (l + d) % 4)) for d in (1, 2, 3)]
    zring += [(row_at(y, 1 - h, k), col_at(x, (l + d) % 4)) for d in (0, 1, 2, 3)]
    partners = zring + [
        (r, col_at(x + 1, l)),
        (r, col_at(x - 1, l)),
        (row_at(y + 1, h, k), c),
        (row_at(y - 1, h, k), c),
        (row_at(y, h, 1 - k), c),
        (r, col_at(x + 2, l)),
        (row_at(y + 2, h, k), c),
    ]
    barrier = pltpu.get_barrier_semaphore()
    for p in partners:
        pl.semaphore_signal(barrier, inc=1, device_id=p, device_id_type=MESH)

    @pl.when(moves)
    def _():
        pl.semaphore_signal(barrier, inc=1, device_id=(mine, r), device_id_type=MESH)

    scale = jnp.sqrt(jnp.full((8, 128), weight[r], F32) / TOK)[0:1, 0:1]
    cs[r] = (act[...].astype(F32) * scale).astype(BF)

    @pl.when(c == 0)
    def _():
        ss[r] = cs[r, 0:512]

    @pl.when(stays)
    def _():
        rs[r] = cs[r]

    pl.semaphore_wait(barrier, jnp.where(stays, len(partners), len(partners) + 1))

    pending = []

    def copy(src, dst, recv, target, cond=None):
        d = pltpu.make_async_remote_copy(
            src_ref=src,
            dst_ref=dst,
            send_sem=send.at[len(pending)],
            recv_sem=recv,
            device_id=target,
            device_id_type=MESH,
        )
        if cond is None:
            d.start()
        else:
            pl.when(cond)(d.start)
        pending.append((cond, src))

    def send_c(t, target):
        copy(cs.at[t], cs.at[t], crecv.at[t], target)

    def send_r(t, target):
        copy(rs.at[t], rs.at[t], rrecv.at[t], target)

    def s_ref(t, half):
        return ss.at[t, pl.ds(*PIECES[half])]

    def send_s(t, half, target, cond=None):
        copy(s_ref(t, half), s_ref(t, half), srecv.at[t, half], target, cond)

    def arrived(ref, sem):
        pltpu.make_async_remote_copy(
            src_ref=ref, dst_ref=ref, send_sem=send.at[0], recv_sem=sem, device_id=(r, c), device_id_type=MESH
        ).wait_recv()

    def wait_c(t):
        arrived(cs.at[t], crecv.at[t])

    def wait_r(t):
        arrived(rs.at[t], rrecv.at[t])

    def wait_s(t, half):
        arrived(s_ref(t, half), srecv.at[t, half])

    twin = row_at(y, 1 - h, k)
    up, down = row_at(y + 1, h, k), row_at(y - 1, h, k)
    right, left = col_at(x + 1, l), col_at(x - 1, l)
    other = row_at(y, h, 1 - k)

    down_line = [jnp.maximum(l - d, 0) for d in range(4)]
    up_line = [jnp.minimum(l + d, 3) for d in range(4)]
    minus = [slot_at(x, ll) for ll in down_line]
    plus = [slot_at(x, ll) for ll in up_line]
    minus_on_left = [slot_at(x - 1, ll) for ll in down_line]
    minus_on_right = [slot_at(x + 1, ll) for ll in down_line]
    plus_on_left = [slot_at(x - 1, ll) for ll in up_line]
    plus_on_right = [slot_at(x + 1, ll) for ll in up_line]
    from_minus = [l >= d for d in range(4)]
    from_plus = [l + d <= 3 for d in range(4)]
    pass_plus = [jnp.logical_and(l >= d, l <= 2) for d in range(4)]
    pass_minus = [jnp.logical_and(l + d <= 3, l >= 1) for d in range(4)]
    odd_slot = [(c + d) % 2 == 1 for d in range(4)]
    even_slot = [(c + d) % 2 == 0 for d in range(4)]
    side = [
        [jnp.logical_and(v, p) for v, p in zip(f, par)]
        for f in (from_minus, from_plus)
        for par in (even_slot, odd_slot)
    ]
    before, after = 4 * x + down_line[1], 4 * x + up_line[1]
    below = [row_at(y - 1, hh, k) for hh in range(2)]
    above = [row_at(y + 1, hh, k) for hh in range(2)]
    beyond = [row_at(y + 2, hh, k) for hh in range(2)]
    across = [row_at(y + d, hh, 1 - k) for d in range(4) for hh in range(2)]
    own_two = (r, twin)
    far_row, far_col = row_at(y + 2, h, k), col_at(x + 2, l)

    at_l0 = l == 0
    off_l0 = l != 0
    source = c == 0
    passes_z = jnp.logical_and(at_l0, x != 0)

    def s_x(half):
        for target in (right, left, far_col):
            send_s(r, half, (r, target), source)

    def s_z(half):
        pl.when(passes_z)(lambda: wait_s(r, half))
        for p in zring:
            send_s(r, half, p, at_l0)

    def s_y(half):
        pl.when(off_l0)(lambda: wait_s(r, half))
        wait_s(twin, half)
        for t in own_two:
            send_s(t, half, (up, c))
            send_s(t, half, (down, c))
            send_s(t, half, (far_row, c))
        for t in own_two:
            send_s(t, half, (other, c))

    def s_core(half):
        for group in (below, above, beyond):
            for t in group:
                wait_s(t, half)
                send_s(t, half, (other, c))

    def s_end(half):
        for t in across:
            wait_s(t, half)

    def r_first():
        pl.when(moves)(lambda: wait_r(mine))
        copy(rs.at[mine], rs.at[mine], rrecv.at[mine], (r, after), pass_plus[0])
        copy(rs.at[mine], rs.at[mine], rrecv.at[mine], (r, before), pass_minus[0])
        send_r(mine, (r, right))
        send_r(mine, (r, left))

    def r_line(d):
        def from_before():
            wait_r(minus[d])

        def from_after():
            wait_r(plus[d])

        pl.when(from_minus[d])(from_before)
        pl.when(from_plus[d])(from_after)
        copy(rs.at[minus[d]], rs.at[minus[d]], rrecv.at[minus[d]], (r, after), pass_plus[d])
        copy(rs.at[plus[d]], rs.at[plus[d]], rrecv.at[plus[d]], (r, before), pass_minus[d])
        for target in (right, left):
            copy(rs.at[minus[d]], rs.at[minus[d]], rrecv.at[minus[d]], (r, target), from_minus[d])
            copy(rs.at[plus[d]], rs.at[plus[d]], rrecv.at[plus[d]], (r, target), from_plus[d])

    def r_ring(d):
        ways = [(from_minus, minus_on_left, minus_on_right, 0)]
        if d > 0:
            ways.append((from_plus, plus_on_left, plus_on_right, 2))
        for there, on_left, on_right, at in ways:

            def both():
                wait_r(on_left[d])
                wait_r(on_right[d])

            pl.when(there[d])(both)
            copy(rs.at[on_left[d]], rs.at[on_left[d]], rrecv.at[on_left[d]], (r, right), side[at][d])
            copy(rs.at[on_right[d]], rs.at[on_right[d]], rrecv.at[on_right[d]], (r, left), side[at + 1][d])

    def c_first():
        send_c(r, (twin, c))
        send_c(r, (up, c))
        send_c(r, (down, c))
        send_c(r, (other, c))

    def c_twin():
        wait_c(twin)
        send_c(twin, (up, c))
        send_c(twin, (down, c))
        send_c(twin, (other, c))

    def c_pass():
        for hh in range(2):
            wait_c(below[hh])
            wait_c(above[hh])
        send_c(below[0], (up, c))
        send_c(above[1], (down, c))
        for hh in range(2):
            send_c(below[hh], (other, c))
            send_c(above[hh], (other, c))

    def c_far():
        for hh in range(2):
            wait_c(beyond[hh])
            send_c(beyond[hh], (other, c))

    def bring(piece):
        base, wide = PIECES[piece]
        p, w = base // 128, wide // 128
        s_old = jnp.concatenate([ss[t, 0:base] for t in range(16)], 1)
        s_new = jnp.concatenate([ss[t, base : base + wide] for t in range(16)], 1)
        g_new = dot_nt(s_new, s_new)
        i = lax.broadcasted_iota(jnp.int32, (wide, wide), 0)
        j = lax.broadcasted_iota(jnp.int32, (wide, wide), 1)
        m_new = jnp.where(i == j, g_new + ridge_value, alpha_scale * g_new)
        one = jnp.where(i == j, 1.0, 0.0)
        if base:
            g_mix = alpha_scale * dot_nt(s_old, s_new)
            w_old = jnp.concatenate([m4[0 : 16 * p, 4 + t].reshape(base, 128) for t in range(p)], 1)
            wh, wm, wl = split3(w_old)
            u = jnp.dot(
                jnp.concatenate([wh, wh, wh, wm, wm, wl], 1), six_right(g_mix), preferred_element_type=F32
            )
            below_it = dot_tn(six_left(u), six_right(jnp.concatenate([u, w_old], 1)))
            m_new = m_new - below_it[:, :wide]
        rows = slice(16 * p, 16 * (p + w))
        for t in range(w):
            cut = slice(128 * t, 128 * t + 128)
            if base:
                m4[0 : 16 * p, p + t] = u[:, cut].reshape(16 * p, 8, 128)
            m4[rows, p + t] = m_new[:, cut].reshape(16 * w, 8, 128)
            m4[rows, 4 + p + t] = one[:, cut].reshape(16 * w, 8, 128)
        for t in range(p):
            m4[rows, 4 + t] = (-below_it[:, wide + 128 * t : wide + 128 * t + 128]).reshape(16 * w, 8, 128)

    s_x(0)
    copy(cs.at[r], rs.at[r], rrecv.at[r], (goes_row, goes_col), moves)
    s_x(1)
    s_x(2)
    s_z(0)
    s_z(1)
    s_z(2)
    s_y(0)
    r_first()
    s_core(0)
    s_y(1)
    s_end(0)

    hooks = [
        (0, lambda: bring(0)),
        (0, lambda: s_y(2)),
        (1, c_first),
        (2, lambda: r_line(1)),
        (3, lambda: s_core(1)),
        (5, lambda: r_ring(0)),
        (6, lambda: r_line(2)),
        (7, lambda: s_core(2)),
        (8, lambda: s_end(1)),
        (8, lambda: bring(1)),
        (9, lambda: r_ring(1)),
        (11, lambda: r_line(3)),
        (13, c_twin),
        (15, lambda: r_ring(2)),
        (16, lambda: s_end(2)),
        (16, lambda: bring(2)),
        (19, c_pass),
        (20, lambda: r_ring(3)),
        (25, c_far),
    ]

    m4[...] = jnp.zeros_like(m4)
    factor(m4, hooks)

    for d in range(4):
        for hh in range(2):
            wait_c(row_at(y + d, hh, 1 - k))
    s_again = jnp.concatenate([ss[t] for t in range(16)], 1)
    c_all = jnp.concatenate([cs[t] for t in range(16)], 1)
    for n in range(2):
        yc[:, 256 * n : 256 * n + 256] = alpha_scale * dot_nt(c_all, s_again[256 * n : 256 * n + 256])

    wide = [jnp.concatenate([m4[pl.ds(16 * b, 16), 4 + t].reshape(128, 128) for b in range(4)], 0) for t in range(4)]
    w_high, w_low = two(jnp.concatenate(wide, 1))
    w_right = jnp.concatenate([w_high, w_low, w_high], 1)

    def solve(y_ref, p_ref):
        y_high, y_low = two(y_ref[...])
        p_ref[...] = dot_nt(jnp.concatenate([y_high, y_high, y_low], 1), w_right)

    solve(yc, pc)

    for ll in range(4):
        wait_r(slot_at(x + 2, ll))
    r_all = jnp.concatenate([rs[t] for t in range(16)], 1)
    for n in range(2):
        yr[:, 256 * n : 256 * n + 256] = alpha_scale * dot_nt(r_all, s_again[256 * n : 256 * n + 256])
    solve(yr, pr)

    w_mine = jnp.concatenate([m4[pl.ds(4 * c, 4), 4 + t].reshape(32, 128) for t in range(4)], 1)
    wm_high, wm_low = two(w_mine)
    y_high, y_low = two(yr[...])
    panels[...] = dot_nt(
        jnp.concatenate([wm_high, wm_low, wm_high], 1), jnp.concatenate([y_high, y_high, y_low], 1)
    )

    @pl.when(r == 0)
    def _():
        i = lax.broadcasted_iota(jnp.int32, (32, 128), 0) + 32 * c
        for t in range(4):
            u = m4[pl.ds(4 * c, 4), t].reshape(32, 128)
            j = lax.broadcasted_iota(jnp.int32, (32, 128), 1) + 128 * t
            panels[:, 128 * t : 128 * t + 128] = jnp.where(j >= i, u, 0.0)

    pr_high, pr_low = two(pr[...])
    pc_high, pc_low = two(pc[...])
    p_left = jnp.concatenate([pr_high, pr_high, pr_low], 1)
    p_right = jnp.concatenate([pc_high, pc_low, pc_high], 1)
    row0 = jnp.where(r == 0, 512, 0)
    col0 = jnp.where(c == 0, 512, 0)
    for n in range(0, 800, 256):
        w = min(256, 800 - n)
        g = dot_nt(r_all, c_all[n : n + w])
        pp = dot_nt(p_left, p_right[n : n + w])
        i = lax.broadcasted_iota(jnp.int32, (800, w), 0)
        j = lax.broadcasted_iota(jnp.int32, (800, w), 1) + n
        m = jnp.where(i == jnp.where(r == c, j, -1), g + ridge_value, alpha_scale * g) - pp
        trailing[:, n : n + w] = jnp.where(jnp.logical_and(i >= row0, j >= col0), m, 0.0)

    for at, (cond, src) in enumerate(pending):
        sent = pltpu.make_async_remote_copy(
            src_ref=src, dst_ref=src, send_sem=send.at[at], recv_sem=crecv.at[0], device_id=(other, c), device_id_type=MESH
        ).wait_send
        if cond is None:
            sent()
        else:
            pl.when(cond)(sent)


def body(activations, task_weight):
    vmem = pl.BlockSpec(memory_space=pltpu.VMEM)
    trailing, panels = pl.pallas_call(
        kernel,
        out_shape=(
            jax.ShapeDtypeStruct((800, 800), F32),
            jax.ShapeDtypeStruct((32, 800), F32),
        ),
        in_specs=[vmem, pl.BlockSpec(memory_space=pltpu.SMEM)],
        out_specs=(vmem, vmem),
        scratch_shapes=[
            pltpu.VMEM((16, 800, 128), BF),
            pltpu.VMEM((16, 800, 128), BF),
            pltpu.VMEM((16, 512, 128), BF),
            pltpu.VMEM((64, 8, 8, 128), F32),
            pltpu.VMEM((800, 512), F32),
            pltpu.VMEM((800, 512), F32),
            pltpu.VMEM((800, 512), F32),
            pltpu.VMEM((800, 512), F32),
            pltpu.SemaphoreType.DMA((128,)),
            pltpu.SemaphoreType.DMA((16,)),
            pltpu.SemaphoreType.DMA((16,)),
            pltpu.SemaphoreType.DMA((16, 3)),
        ],
        compiler_params=pltpu.CompilerParams(
            collective_id=0, has_side_effects=True, vmem_limit_bytes=60 << 20
        ),
    )(activations.T, task_weight)
    return trailing, panels.T


def solution(mesh):
    placed = (P("row", "col"), P())
    return jax.shard_map(
        body,
        mesh=mesh,
        in_specs=placed,
        out_specs=(P("row", "col"), P("row", "col")),
        check_vma=False,
    )
```

```python
import jax
import jax.numpy as jnp
from jax import lax
from jax.experimental import pallas as pl
from jax.experimental.pallas import tpu as pltpu
from jax.sharding import PartitionSpec as P

TOK = 128
PANEL = 256
LEAF = 16
PIECES = ((0, 128), (128, 128), (256, 256))

alpha_scale = 0.9
ridge_value = 0.2

F32 = jnp.float32
BF = jnp.bfloat16
MESH = pl.DeviceIdType.MESH


def dot_nt(a, b):
    return lax.dot_general(a, b, (((1,), (1,)), ((), ())), preferred_element_type=F32)


def dot_tn(a, b):
    return lax.dot_general(a, b, (((0,), (0,)), ((), ())), preferred_element_type=F32)


def split3(x):
    high = x.astype(BF)
    rest = x - high.astype(F32)
    mid = rest.astype(BF)
    low = (rest - mid.astype(F32)).astype(BF)
    return high, mid, low


def six_left(x):
    h, m, l = split3(x)
    return jnp.concatenate([h, h, h, m, m, l], 0)


def six_right(x):
    h, m, l = split3(x)
    return jnp.concatenate([h, m, l, h, m, h], 0)


def two(x):
    high = x.astype(BF)
    return high, (x - high.astype(F32)).astype(BF)


def sub_cast(x, s):
    return jnp.broadcast_to(x[s : s + 1, :], (8, 128))


def lane_cast(x, k):
    return jnp.broadcast_to(x[:, k : k + 1], (8, 128))


def chain8(s, rows, cols):
    for k in range(8):
        r = lax.rsqrt(s[k, k])
        for j in range(k + 1, 8):
            s[j, k] = s[j, k] * r
        for q in range(k + 1, 8):
            for j in range(q, 8):
                s[j, q] = s[j, q] - s[j, k] * s[q, k]
        rows[k] = rows[k] * r
        for j in range(k + 1, 8):
            rows[j] = rows[j] - s[j, k] * rows[k]
        if cols is not None:
            cols[k] = cols[k] * r
            for q in range(k + 1, 8):
                cols[q] = cols[q] - cols[k] * s[q, k]


def leaf_factor(m4, kb, leaf):
    i0 = kb * 16 + 2 * leaf
    o = LEAF * leaf
    d0 = m4[i0, kb]
    d1 = m4[i0 + 1, kb]
    s = {}
    for k in range(8):
        column = lane_cast(d0, o + k)
        for j in range(k, 8):
            s[j, k] = sub_cast(column, j)
    cols = [lane_cast(d1, o + k) for k in range(16)]
    upper = [m4[i0, :, q, :] for q in range(8)]
    first = cols[:8]
    chain8(s, upper, first)
    for q in range(8):
        m4[i0, :, q, :] = upper[q]
    lower = [m4[i0 + 1, :, q, :] for q in range(8)]
    second = cols[8:]
    for k in range(8):
        t = [sub_cast(first[k], q) for q in range(8)]
        for q in range(8):
            second[q] = second[q] - first[k] * t[q]
        for q in range(8):
            lower[q] = lower[q] - t[q] * upper[k]
    s = {}
    for k in range(8):
        for j in range(k, 8):
            s[j, k] = sub_cast(second[k], j)
    chain8(s, lower, None)
    for q in range(8):
        m4[i0 + 1, :, q, :] = lower[q]


def inner_update(m4, kb, leaf):
    i0 = kb * 16 + 2 * leaf
    u = m4[pl.ds(i0, 2), pl.ds(kb, 5)]
    tiles = [u[:, t].reshape(16, 128) for t in range(5)]
    left = six_left(tiles[0])[:, LEAF * (leaf + 1) :]
    up = dot_tn(left, six_right(jnp.concatenate(tiles, 1)))
    for q in range((7 - leaf) * 2):
        for t in range(5):
            m4[i0 + 2 + q, kb + t] = (
                m4[i0 + 2 + q, kb + t] - up[8 * q : 8 * q + 8, 128 * t : 128 * t + 128]
            )


def rest_update(m4, kb, b):
    left = six_left(m4[pl.ds(kb * 16, 16), b].reshape(128, 128))
    for half in range(2):
        w = jnp.concatenate(
            [m4[pl.ds(kb * 16, 16), kb + 1 + 2 * half + t].reshape(128, 128) for t in range(2)], 1
        )
        up = dot_tn(left, six_right(w))
        for t in range(2):
            tt = kb + 1 + 2 * half + t
            m4[pl.ds(b * 16, 16), tt] = m4[pl.ds(b * 16, 16), tt] - up[
                :, 128 * t : 128 * t + 128
            ].reshape(16, 8, 128)


def factor(m4, hooks, beside):
    def early(kb, _):
        for leaf in range(8):
            for at, run in hooks:
                if at < 16 and at % 8 == leaf:
                    pl.when(kb == at // 8)(run)
            leaf_factor(m4, kb, leaf)
            if leaf < 7:
                inner_update(m4, kb, leaf)
        return 0

    lax.fori_loop(0, 2, early, 0)
    for kb in (2, 3):
        for leaf in range(8):
            for at, run in hooks:
                if at == 8 * kb + leaf:
                    run()
            for at, run in beside:
                if at == 8 * kb + leaf:
                    run()
            leaf_factor(m4, kb, leaf)
            if leaf < 7:
                inner_update(m4, kb, leaf)
        if kb == 2:
            rest_update(m4, 2, 3)


def kernel(act, weight, trailing, panels, cs, rs, ss, m4, yr, yc, pr, pc, send, crecv, rrecv, srecv):
    r = lax.axis_index("row")
    c = lax.axis_index("col")
    y, h, k = r // 4, (r // 2) % 2, r % 2
    x, l = c // 4, c % 4

    def row_at(yy, hh, kk):
        return 4 * ((yy + 4) % 4) + 2 * hh + kk

    def col_at(xx, ll):
        return 4 * ((xx + 8) % 4) + ll

    def slot_at(xx, ll):
        return 4 * ((2 * y - xx + 8) % 4) + 2 * ((ll // 2 + k + h) % 2) + ll % 2

    mine = slot_at(x, l)
    goes_row = c
    goes_col = col_at(2 * x - y, 2 * ((h + l // 2 + l % 2) % 2) + k)
    moves = jnp.logical_or(goes_row != r, goes_col != c)
    stays = jnp.logical_not(moves)

    zring = [(r, col_at(x, (l + d) % 4)) for d in (1, 2, 3)]
    zring += [(row_at(y, 1 - h, k), col_at(x, (l + d) % 4)) for d in (0, 1, 2, 3)]
    partners = zring + [
        (r, col_at(x + 1, l)),
        (r, col_at(x - 1, l)),
        (row_at(y + 1, h, k), c),
        (row_at(y - 1, h, k), c),
        (row_at(y, h, 1 - k), c),
        (r, col_at(x + 2, l)),
        (row_at(y + 2, h, k), c),
    ]
    barrier = pltpu.get_barrier_semaphore()
    for p in partners:
        pl.semaphore_signal(barrier, inc=1, device_id=p, device_id_type=MESH)

    @pl.when(moves)
    def _():
        pl.semaphore_signal(barrier, inc=1, device_id=(mine, r), device_id_type=MESH)

    scale = jnp.sqrt(jnp.full((8, 128), weight[r], F32) / TOK)[0:1, 0:1]
    cs[r] = (act[...].astype(F32) * scale).astype(BF)

    @pl.when(c == 0)
    def _():
        ss[r] = cs[r, 0:512]

    @pl.when(stays)
    def _():
        rs[r] = cs[r]

    pl.semaphore_wait(barrier, jnp.where(stays, len(partners), len(partners) + 1))

    pending = []

    def copy(src, dst, recv, target, cond=None):
        d = pltpu.make_async_remote_copy(
            src_ref=src,
            dst_ref=dst,
            send_sem=send.at[len(pending)],
            recv_sem=recv,
            device_id=target,
            device_id_type=MESH,
        )
        if cond is None:
            d.start()
        else:
            pl.when(cond)(d.start)
        pending.append((cond, src))

    def send_c(t, target):
        copy(cs.at[t], cs.at[t], crecv.at[t], target)

    def send_r(t, target):
        copy(rs.at[t], rs.at[t], rrecv.at[t], target)

    def s_ref(t, half):
        return ss.at[t, pl.ds(*PIECES[half])]

    def send_s(t, half, target, cond=None):
        copy(s_ref(t, half), s_ref(t, half), srecv.at[t, half], target, cond)

    def arrived(ref, sem):
        pltpu.make_async_remote_copy(
            src_ref=ref, dst_ref=ref, send_sem=send.at[0], recv_sem=sem, device_id=(r, c), device_id_type=MESH
        ).wait_recv()

    def wait_c(t):
        arrived(cs.at[t], crecv.at[t])

    def wait_r(t):
        arrived(rs.at[t], rrecv.at[t])

    def wait_s(t, half):
        arrived(s_ref(t, half), srecv.at[t, half])

    twin = row_at(y, 1 - h, k)
    up, down = row_at(y + 1, h, k), row_at(y - 1, h, k)
    right, left = col_at(x + 1, l), col_at(x - 1, l)
    other = row_at(y, h, 1 - k)

    down_line = [jnp.maximum(l - d, 0) for d in range(4)]
    up_line = [jnp.minimum(l + d, 3) for d in range(4)]
    minus = [slot_at(x, ll) for ll in down_line]
    plus = [slot_at(x, ll) for ll in up_line]
    minus_on_left = [slot_at(x - 1, ll) for ll in down_line]
    minus_on_right = [slot_at(x + 1, ll) for ll in down_line]
    plus_on_left = [slot_at(x - 1, ll) for ll in up_line]
    plus_on_right = [slot_at(x + 1, ll) for ll in up_line]
    from_minus = [l >= d for d in range(4)]
    from_plus = [l + d <= 3 for d in range(4)]
    pass_plus = [jnp.logical_and(l >= d, l <= 2) for d in range(4)]
    pass_minus = [jnp.logical_and(l + d <= 3, l >= 1) for d in range(4)]
    odd_slot = [(c + d) % 2 == 1 for d in range(4)]
    even_slot = [(c + d) % 2 == 0 for d in range(4)]
    side = [
        [jnp.logical_and(v, p) for v, p in zip(f, par)]
        for f in (from_minus, from_plus)
        for par in (even_slot, odd_slot)
    ]
    before, after = 4 * x + down_line[1], 4 * x + up_line[1]
    below = [row_at(y - 1, hh, k) for hh in range(2)]
    above = [row_at(y + 1, hh, k) for hh in range(2)]
    beyond = [row_at(y + 2, hh, k) for hh in range(2)]
    across = [row_at(y + d, hh, 1 - k) for d in range(4) for hh in range(2)]
    own_two = (r, twin)
    opposite = [slot_at(x + 2, ll) for ll in range(4)]
    far_row, far_col = row_at(y + 2, h, k), col_at(x + 2, l)

    at_l0 = l == 0
    off_l0 = l != 0
    source = c == 0
    passes_z = jnp.logical_and(at_l0, x != 0)

    def s_x(half):
        for target in (right, left, far_col):
            send_s(r, half, (r, target), source)

    def s_z(half):
        pl.when(passes_z)(lambda: wait_s(r, half))
        for p in zring:
            send_s(r, half, p, at_l0)

    def s_y(half):
        pl.when(off_l0)(lambda: wait_s(r, half))
        wait_s(twin, half)
        for t in own_two:
            send_s(t, half, (up, c))
            send_s(t, half, (down, c))
            send_s(t, half, (far_row, c))
        for t in own_two:
            send_s(t, half, (other, c))

    def s_core(half):
        for group in (below, above, beyond):
            for t in group:
                wait_s(t, half)
                send_s(t, half, (other, c))

    def s_end(half):
        for t in across:
            wait_s(t, half)

    def r_first():
        pl.when(moves)(lambda: wait_r(mine))
        copy(rs.at[mine], rs.at[mine], rrecv.at[mine], (r, after), pass_plus[0])
        copy(rs.at[mine], rs.at[mine], rrecv.at[mine], (r, before), pass_minus[0])
        send_r(mine, (r, right))
        send_r(mine, (r, left))

    def r_line(d):
        def from_before():
            wait_r(minus[d])

        def from_after():
            wait_r(plus[d])

        pl.when(from_minus[d])(from_before)
        pl.when(from_plus[d])(from_after)
        copy(rs.at[minus[d]], rs.at[minus[d]], rrecv.at[minus[d]], (r, after), pass_plus[d])
        copy(rs.at[plus[d]], rs.at[plus[d]], rrecv.at[plus[d]], (r, before), pass_minus[d])
        for target in (right, left):
            copy(rs.at[minus[d]], rs.at[minus[d]], rrecv.at[minus[d]], (r, target), from_minus[d])
            copy(rs.at[plus[d]], rs.at[plus[d]], rrecv.at[plus[d]], (r, target), from_plus[d])

    def r_ring(d):
        ways = [(from_minus, minus_on_left, minus_on_right, 0)]
        if d > 0:
            ways.append((from_plus, plus_on_left, plus_on_right, 2))
        for there, on_left, on_right, at in ways:

            def both():
                wait_r(on_left[d])
                wait_r(on_right[d])

            pl.when(there[d])(both)
            copy(rs.at[on_left[d]], rs.at[on_left[d]], rrecv.at[on_left[d]], (r, right), side[at][d])
            copy(rs.at[on_right[d]], rs.at[on_right[d]], rrecv.at[on_right[d]], (r, left), side[at + 1][d])

    def c_first():
        send_c(r, (twin, c))
        send_c(r, (up, c))
        send_c(r, (down, c))
        send_c(r, (other, c))

    def c_twin():
        wait_c(twin)
        send_c(twin, (up, c))
        send_c(twin, (down, c))
        send_c(twin, (other, c))

    def c_pass():
        for hh in range(2):
            wait_c(below[hh])
            wait_c(above[hh])
        send_c(below[0], (up, c))
        send_c(above[1], (down, c))
        for hh in range(2):
            send_c(below[hh], (other, c))
            send_c(above[hh], (other, c))

    def c_far():
        for hh in range(2):
            wait_c(beyond[hh])
            send_c(beyond[hh], (other, c))

    def c_across(d):
        for t in across[2 * d : 2 * d + 2]:
            wait_c(t)

    def r_end():
        for t in opposite:
            wait_r(t)

    def bring(piece):
        base, wide = PIECES[piece]
        p, w = base // 128, wide // 128
        s_old = jnp.concatenate([ss[t, 0:base] for t in range(16)], 1)
        s_new = jnp.concatenate([ss[t, base : base + wide] for t in range(16)], 1)
        g_new = dot_nt(s_new, s_new)
        i = lax.broadcasted_iota(jnp.int32, (wide, wide), 0)
        j = lax.broadcasted_iota(jnp.int32, (wide, wide), 1)
        m_new = jnp.where(i == j, g_new + ridge_value, alpha_scale * g_new)
        one = jnp.where(i == j, 1.0, 0.0)
        if base:
            g_mix = alpha_scale * dot_nt(s_old, s_new)
            w_old = jnp.concatenate([m4[0 : 16 * p, 4 + t].reshape(base, 128) for t in range(p)], 1)
            wh, wm, wl = split3(w_old)
            u = jnp.dot(
                jnp.concatenate([wh, wh, wh, wm, wm, wl], 1), six_right(g_mix), preferred_element_type=F32
            )
            below_it = dot_tn(six_left(u), six_right(jnp.concatenate([u, w_old], 1)))
            m_new = m_new - below_it[:, :wide]
        rows = slice(16 * p, 16 * (p + w))
        for t in range(w):
            cut = slice(128 * t, 128 * t + 128)
            if base:
                m4[0 : 16 * p, p + t] = u[:, cut].reshape(16 * p, 8, 128)
            m4[rows, p + t] = m_new[:, cut].reshape(16 * w, 8, 128)
            m4[rows, 4 + p + t] = one[:, cut].reshape(16 * w, 8, 128)
        for t in range(p):
            m4[rows, 4 + t] = (-below_it[:, wide + 128 * t : wide + 128 * t + 128]).reshape(16 * w, 8, 128)

    s_x(0)
    copy(cs.at[r], rs.at[r], rrecv.at[r], (goes_row, goes_col), moves)
    s_x(1)
    s_x(2)
    s_z(0)
    s_z(1)
    s_z(2)
    s_y(0)
    r_first()
    s_core(0)
    s_y(1)
    s_end(0)

    hooks = [
        (0, lambda: bring(0)),
        (0, lambda: s_y(2)),
        (1, c_first),
        (2, lambda: r_line(1)),
        (3, lambda: s_core(1)),
        (5, lambda: r_ring(0)),
        (6, lambda: r_line(2)),
        (7, lambda: s_core(2)),
        (8, lambda: s_end(1)),
        (8, lambda: bring(1)),
        (9, lambda: r_ring(1)),
        (11, lambda: r_line(3)),
        (13, c_twin),
        (15, lambda: r_ring(2)),
        (16, lambda: s_end(2)),
        (16, lambda: bring(2)),
        (19, c_pass),
        (20, lambda: r_ring(3)),
        (17, lambda: c_across(0)),
        (22, lambda: c_across(1)),
        (23, lambda: c_across(3)),
        (25, c_far),
        (28, lambda: c_across(2)),
        (30, r_end),
    ]

    m4[...] = jnp.zeros_like(m4)

    def group(slab, total, task_row, start):
        tasks = [4 * task_row + q for q in range(4)]
        add = dot_nt(
            jnp.concatenate([slab[t] for t in tasks], 1), jnp.concatenate([ss[t] for t in tasks], 1)
        )
        total[...] = add if start else total[...] + add

    group_own, group_left, group_right, group_far = [(2 * y - xx + 8) % 4 for xx in (x, x - 1, x + 1, x + 2)]
    y_down, y_up, y_far = (y + 3) % 4, (y + 1) % 4, (y + 2) % 4
    beside = [
        (17, lambda: group(rs, yr, group_own, True)),
        (18, lambda: group(cs, yc, y, True)),
        (21, lambda: group(rs, yr, group_left, False)),
        (22, lambda: group(rs, yr, group_right, False)),
        (23, lambda: group(cs, yc, y_down, False)),
        (24, lambda: group(cs, yc, y_up, False)),
        (29, lambda: group(cs, yc, y_far, False)),
        (31, lambda: group(rs, yr, group_far, False)),
    ]
    factor(m4, hooks, beside)

    wide = [jnp.concatenate([m4[pl.ds(16 * b, 16), 4 + t].reshape(128, 128) for b in range(4)], 0) for t in range(4)]
    w_high, w_low = two(jnp.concatenate(wide, 1))

    def solve(y_ref):
        y_high, y_low = two(alpha_scale * y_ref[...])
        parts = []
        for n in (256, 512):
            yh, yl = y_high[:, :n], y_low[:, :n]
            wh, wl = w_high[n - 256 : n, :n], w_low[n - 256 : n, :n]
            parts.append(
                two(dot_nt(jnp.concatenate([yh, yh, yl], 1), jnp.concatenate([wh, wl, wh], 1)))
            )
        return [jnp.concatenate([p[q] for p in parts], 1) for q in range(2)]

    pc_high, pc_low = solve(yc)
    pc[...] = jnp.concatenate([pc_high, pc_low, pc_high], 1)
    pr_high, pr_low = solve(yr)
    pr[...] = jnp.concatenate([pr_high, pr_high, pr_low], 1)
    c_all = jnp.concatenate([cs[t] for t in range(16)], 1)
    r_all = jnp.concatenate([rs[t] for t in range(16)], 1)

    w_mine = jnp.concatenate([m4[pl.ds(4 * c, 4), 4 + t].reshape(32, 128) for t in range(4)], 1)
    wm_high, wm_low = two(w_mine)
    y_high, y_low = two(alpha_scale * yr[...])
    panels[...] = dot_nt(
        jnp.concatenate([wm_high, wm_low, wm_high], 1), jnp.concatenate([y_high, y_high, y_low], 1)
    )

    @pl.when(r == 0)
    def _():
        i = lax.broadcasted_iota(jnp.int32, (32, 128), 0) + 32 * c
        for t in range(4):
            u = m4[pl.ds(4 * c, 4), t].reshape(32, 128)
            j = lax.broadcasted_iota(jnp.int32, (32, 128), 1) + 128 * t
            panels[:, 128 * t : 128 * t + 128] = jnp.where(j >= i, u, 0.0)

    p_left, p_right = pr[...], pc[...]
    row0 = jnp.where(r == 0, 512, 0)
    col0 = jnp.where(c == 0, 512, 0)
    for n in range(0, 800, 256):
        w = min(256, 800 - n)
        g = dot_nt(r_all, c_all[n : n + w])
        pp = dot_nt(p_left, p_right[n : n + w])
        i = lax.broadcasted_iota(jnp.int32, (800, w), 0)
        j = lax.broadcasted_iota(jnp.int32, (800, w), 1) + n
        m = jnp.where(i == jnp.where(r == c, j, -1), g + ridge_value, alpha_scale * g) - pp
        trailing[:, n : n + w] = jnp.where(jnp.logical_and(i >= row0, j >= col0), m, 0.0)

    for at, (cond, src) in enumerate(pending):
        sent = pltpu.make_async_remote_copy(
            src_ref=src, dst_ref=src, send_sem=send.at[at], recv_sem=crecv.at[0], device_id=(other, c), device_id_type=MESH
        ).wait_send
        if cond is None:
            sent()
        else:
            pl.when(cond)(sent)


def body(activations, task_weight):
    vmem = pl.BlockSpec(memory_space=pltpu.VMEM)
    trailing, panels = pl.pallas_call(
        kernel,
        out_shape=(
            jax.ShapeDtypeStruct((800, 800), F32),
            jax.ShapeDtypeStruct((32, 800), F32),
        ),
        in_specs=[vmem, pl.BlockSpec(memory_space=pltpu.SMEM)],
        out_specs=(vmem, vmem),
        scratch_shapes=[
            pltpu.VMEM((16, 800, 128), BF),
            pltpu.VMEM((16, 800, 128), BF),
            pltpu.VMEM((16, 512, 128), BF),
            pltpu.VMEM((64, 8, 8, 128), F32),
            pltpu.VMEM((800, 512), F32),
            pltpu.VMEM((800, 512), F32),
            pltpu.VMEM((800, 1536), BF),
            pltpu.VMEM((800, 1536), BF),
            pltpu.SemaphoreType.DMA((128,)),
            pltpu.SemaphoreType.DMA((16,)),
            pltpu.SemaphoreType.DMA((16,)),
            pltpu.SemaphoreType.DMA((16, 3)),
        ],
        compiler_params=pltpu.CompilerParams(
            collective_id=0, has_side_effects=True, vmem_limit_bytes=60 << 20
        ),
    )(activations.T, task_weight)
    return trailing, panels.T


def solution(mesh):
    placed = (P("row", "col"), P())
    return jax.shard_map(
        body,
        mesh=mesh,
        in_specs=placed,
        out_specs=(P("row", "col"), P("row", "col")),
        check_vma=False,
    )
```

```python
import jax
import jax.numpy as jnp
from jax import lax
from jax.experimental import pallas as pl
from jax.experimental.pallas import tpu as pltpu
from jax.sharding import PartitionSpec as P

TOK = 128
PANEL = 256
LEAF = 16
PIECES = ((0, 128), (128, 128), (256, 256))

alpha_scale = 0.9
ridge_value = 0.2

F32 = jnp.float32
BF = jnp.bfloat16
MESH = pl.DeviceIdType.MESH


def dot_nt(a, b):
    return lax.dot_general(a, b, (((1,), (1,)), ((), ())), preferred_element_type=F32)


def dot_tn(a, b):
    return lax.dot_general(a, b, (((0,), (0,)), ((), ())), preferred_element_type=F32)


def split3(x):
    high = x.astype(BF)
    rest = x - high.astype(F32)
    mid = rest.astype(BF)
    low = (rest - mid.astype(F32)).astype(BF)
    return high, mid, low


def six_left(x):
    h, m, l = split3(x)
    return jnp.concatenate([h, h, h, m, m, l], 0)


def six_right(x):
    h, m, l = split3(x)
    return jnp.concatenate([h, m, l, h, m, h], 0)


def two(x):
    high = x.astype(BF)
    return high, (x - high.astype(F32)).astype(BF)


def sub_cast(x, s):
    return jnp.broadcast_to(x[s : s + 1, :], (8, 128))


def lane_cast(x, k):
    return jnp.broadcast_to(x[:, k : k + 1], (8, 128))


def chain8(s, rows, cols):
    for k in range(8):
        r = lax.rsqrt(s[k, k])
        for j in range(k + 1, 8):
            s[j, k] = s[j, k] * r
        for q in range(k + 1, 8):
            for j in range(q, 8):
                s[j, q] = s[j, q] - s[j, k] * s[q, k]
        rows[k] = rows[k] * r
        for j in range(k + 1, 8):
            rows[j] = rows[j] - s[j, k] * rows[k]
        if cols is not None:
            cols[k] = cols[k] * r
            for q in range(k + 1, 8):
                cols[q] = cols[q] - cols[k] * s[q, k]


def leaf_factor(m4, kb, leaf):
    i0 = kb * 16 + 2 * leaf
    o = LEAF * leaf
    d0 = m4[i0, kb]
    d1 = m4[i0 + 1, kb]
    s = {}
    for k in range(8):
        column = lane_cast(d0, o + k)
        for j in range(k, 8):
            s[j, k] = sub_cast(column, j)
    cols = [lane_cast(d1, o + k) for k in range(16)]
    upper = [m4[i0, :, q, :] for q in range(8)]
    first = cols[:8]
    chain8(s, upper, first)
    for q in range(8):
        m4[i0, :, q, :] = upper[q]
    lower = [m4[i0 + 1, :, q, :] for q in range(8)]
    second = cols[8:]
    for k in range(8):
        t = [sub_cast(first[k], q) for q in range(8)]
        for q in range(8):
            second[q] = second[q] - first[k] * t[q]
        for q in range(8):
            lower[q] = lower[q] - t[q] * upper[k]
    s = {}
    for k in range(8):
        for j in range(k, 8):
            s[j, k] = sub_cast(second[k], j)
    chain8(s, lower, None)
    for q in range(8):
        m4[i0 + 1, :, q, :] = lower[q]


def inner_update(m4, kb, leaf):
    i0 = kb * 16 + 2 * leaf
    u = m4[pl.ds(i0, 2), pl.ds(kb, 5)]
    tiles = [u[:, t].reshape(16, 128) for t in range(5)]
    left = six_left(tiles[0])[:, LEAF * (leaf + 1) :]
    up = dot_tn(left, six_right(jnp.concatenate(tiles, 1)))
    for q in range((7 - leaf) * 2):
        for t in range(5):
            m4[i0 + 2 + q, kb + t] = (
                m4[i0 + 2 + q, kb + t] - up[8 * q : 8 * q + 8, 128 * t : 128 * t + 128]
            )


def rest_update(m4, kb, b):
    left = six_left(m4[pl.ds(kb * 16, 16), b].reshape(128, 128))
    for half in range(2):
        w = jnp.concatenate(
            [m4[pl.ds(kb * 16, 16), kb + 1 + 2 * half + t].reshape(128, 128) for t in range(2)], 1
        )
        up = dot_tn(left, six_right(w))
        for t in range(2):
            tt = kb + 1 + 2 * half + t
            m4[pl.ds(b * 16, 16), tt] = m4[pl.ds(b * 16, 16), tt] - up[
                :, 128 * t : 128 * t + 128
            ].reshape(16, 8, 128)


def factor(m4, hooks, beside):
    def early(kb, _):
        for leaf in range(8):
            for at, run in hooks:
                if at < 16 and at % 8 == leaf:
                    pl.when(kb == at // 8)(run)
            leaf_factor(m4, kb, leaf)
            if leaf < 7:
                inner_update(m4, kb, leaf)
        return 0

    lax.fori_loop(0, 2, early, 0)
    for kb in (2, 3):
        for leaf in range(8):
            for at, run in hooks:
                if at == 8 * kb + leaf:
                    run()
            for at, run in beside:
                if at == 8 * kb + leaf:
                    run()
            leaf_factor(m4, kb, leaf)
            if leaf < 7:
                inner_update(m4, kb, leaf)
        if kb == 2:
            rest_update(m4, 2, 3)


def kernel(act, weight, trailing, panels, cs, rs, ss, m4, yr, yc, pr, pc, send, crecv, rrecv, srecv):
    r = lax.axis_index("row")
    c = lax.axis_index("col")
    y, h, k = r // 4, (r // 2) % 2, r % 2
    x, l = c // 4, c % 4

    def row_at(yy, hh, kk):
        return 4 * ((yy + 4) % 4) + 2 * hh + kk

    def col_at(xx, ll):
        return 4 * ((xx + 8) % 4) + ll

    def slot_at(xx, ll):
        return 4 * ((2 * y - xx + 8) % 4) + 2 * ((ll // 2 + k + h) % 2) + ll % 2

    mine = slot_at(x, l)
    goes_row = c
    goes_col = col_at(2 * x - y, 2 * ((h + l // 2 + l % 2) % 2) + k)
    moves = jnp.logical_or(goes_row != r, goes_col != c)
    stays = jnp.logical_not(moves)

    zring = [(r, col_at(x, (l + d) % 4)) for d in (1, 2, 3)]
    zring += [(row_at(y, 1 - h, k), col_at(x, (l + d) % 4)) for d in (0, 1, 2, 3)]
    partners = zring + [
        (r, col_at(x + 1, l)),
        (r, col_at(x - 1, l)),
        (row_at(y + 1, h, k), c),
        (row_at(y - 1, h, k), c),
        (row_at(y, h, 1 - k), c),
        (r, col_at(x + 2, l)),
        (row_at(y + 2, h, k), c),
    ]
    barrier = pltpu.get_barrier_semaphore()
    for p in partners:
        pl.semaphore_signal(barrier, inc=1, device_id=p, device_id_type=MESH)

    @pl.when(moves)
    def _():
        pl.semaphore_signal(barrier, inc=1, device_id=(mine, r), device_id_type=MESH)

    scale = jnp.sqrt(jnp.full((8, 128), weight[r], F32) / TOK)[0:1, 0:1]
    cs[r] = (act[...].astype(F32) * scale).astype(BF)

    @pl.when(c == 0)
    def _():
        ss[r] = cs[r, 0:512]

    @pl.when(stays)
    def _():
        rs[r] = cs[r]

    pl.semaphore_wait(barrier, jnp.where(stays, len(partners), len(partners) + 1))

    pending = []

    def copy(src, dst, recv, target, cond=None):
        d = pltpu.make_async_remote_copy(
            src_ref=src,
            dst_ref=dst,
            send_sem=send.at[len(pending)],
            recv_sem=recv,
            device_id=target,
            device_id_type=MESH,
        )
        if cond is None:
            d.start()
        else:
            pl.when(cond)(d.start)
        pending.append((cond, src))

    def send_c(t, target):
        copy(cs.at[t], cs.at[t], crecv.at[t], target)

    def send_r(t, target):
        copy(rs.at[t], rs.at[t], rrecv.at[t], target)

    def s_ref(t, half):
        return ss.at[t, pl.ds(*PIECES[half])]

    def send_s(t, half, target, cond=None):
        copy(s_ref(t, half), s_ref(t, half), srecv.at[t, half], target, cond)

    def arrived(ref, sem):
        pltpu.make_async_remote_copy(
            src_ref=ref, dst_ref=ref, send_sem=send.at[0], recv_sem=sem, device_id=(r, c), device_id_type=MESH
        ).wait_recv()

    def wait_c(t):
        arrived(cs.at[t], crecv.at[t])

    def wait_r(t):
        arrived(rs.at[t], rrecv.at[t])

    def wait_s(t, half):
        arrived(s_ref(t, half), srecv.at[t, half])

    twin = row_at(y, 1 - h, k)
    up, down = row_at(y + 1, h, k), row_at(y - 1, h, k)
    right, left = col_at(x + 1, l), col_at(x - 1, l)
    other = row_at(y, h, 1 - k)

    down_line = [jnp.maximum(l - d, 0) for d in range(4)]
    up_line = [jnp.minimum(l + d, 3) for d in range(4)]
    minus = [slot_at(x, ll) for ll in down_line]
    plus = [slot_at(x, ll) for ll in up_line]
    minus_on_left = [slot_at(x - 1, ll) for ll in down_line]
    minus_on_right = [slot_at(x + 1, ll) for ll in down_line]
    plus_on_left = [slot_at(x - 1, ll) for ll in up_line]
    plus_on_right = [slot_at(x + 1, ll) for ll in up_line]
    from_minus = [l >= d for d in range(4)]
    from_plus = [l + d <= 3 for d in range(4)]
    pass_plus = [jnp.logical_and(l >= d, l <= 2) for d in range(4)]
    pass_minus = [jnp.logical_and(l + d <= 3, l >= 1) for d in range(4)]
    odd_slot = [(c + d) % 2 == 1 for d in range(4)]
    even_slot = [(c + d) % 2 == 0 for d in range(4)]
    side = [
        [jnp.logical_and(v, p) for v, p in zip(f, par)]
        for f in (from_minus, from_plus)
        for par in (even_slot, odd_slot)
    ]
    before, after = 4 * x + down_line[1], 4 * x + up_line[1]
    below = [row_at(y - 1, hh, k) for hh in range(2)]
    above = [row_at(y + 1, hh, k) for hh in range(2)]
    beyond = [row_at(y + 2, hh, k) for hh in range(2)]
    across = [row_at(y + d, hh, 1 - k) for d in range(4) for hh in range(2)]
    own_two = (r, twin)
    opposite = [slot_at(x + 2, ll) for ll in range(4)]
    far_row, far_col = row_at(y + 2, h, k), col_at(x + 2, l)

    at_l0 = l == 0
    off_l0 = l != 0
    source = c == 0
    passes_z = jnp.logical_and(at_l0, x != 0)

    def s_x(half):
        for target in (right, left, far_col):
            send_s(r, half, (r, target), source)

    def s_z(half):
        pl.when(passes_z)(lambda: wait_s(r, half))
        for p in zring:
            send_s(r, half, p, at_l0)

    def s_y(half):
        pl.when(off_l0)(lambda: wait_s(r, half))
        wait_s(twin, half)
        for t in own_two:
            send_s(t, half, (up, c))
            send_s(t, half, (down, c))
            send_s(t, half, (far_row, c))
        for t in own_two:
            send_s(t, half, (other, c))

    def s_core(half):
        for group in (below, above, beyond):
            for t in group:
                wait_s(t, half)
                send_s(t, half, (other, c))

    def s_end(half):
        for t in across:
            wait_s(t, half)

    def r_first():
        pl.when(moves)(lambda: wait_r(mine))
        copy(rs.at[mine], rs.at[mine], rrecv.at[mine], (r, after), pass_plus[0])
        copy(rs.at[mine], rs.at[mine], rrecv.at[mine], (r, before), pass_minus[0])
        send_r(mine, (r, right))
        send_r(mine, (r, left))

    def r_line(d):
        def from_before():
            wait_r(minus[d])

        def from_after():
            wait_r(plus[d])

        pl.when(from_minus[d])(from_before)
        pl.when(from_plus[d])(from_after)
        copy(rs.at[minus[d]], rs.at[minus[d]], rrecv.at[minus[d]], (r, after), pass_plus[d])
        copy(rs.at[plus[d]], rs.at[plus[d]], rrecv.at[plus[d]], (r, before), pass_minus[d])
        for target in (right, left):
            copy(rs.at[minus[d]], rs.at[minus[d]], rrecv.at[minus[d]], (r, target), from_minus[d])
            copy(rs.at[plus[d]], rs.at[plus[d]], rrecv.at[plus[d]], (r, target), from_plus[d])

    def r_ring(d):
        ways = [(from_minus, minus_on_left, minus_on_right, 0)]
        if d > 0:
            ways.append((from_plus, plus_on_left, plus_on_right, 2))
        for there, on_left, on_right, at in ways:

            def both():
                wait_r(on_left[d])
                wait_r(on_right[d])

            pl.when(there[d])(both)
            copy(rs.at[on_left[d]], rs.at[on_left[d]], rrecv.at[on_left[d]], (r, right), side[at][d])
            copy(rs.at[on_right[d]], rs.at[on_right[d]], rrecv.at[on_right[d]], (r, left), side[at + 1][d])

    def c_first():
        send_c(r, (twin, c))
        send_c(r, (up, c))
        send_c(r, (down, c))
        send_c(r, (other, c))

    def c_twin():
        wait_c(twin)
        send_c(twin, (up, c))
        send_c(twin, (down, c))
        send_c(twin, (other, c))

    def c_pass():
        for hh in range(2):
            wait_c(below[hh])
            wait_c(above[hh])
        send_c(below[0], (up, c))
        send_c(above[1], (down, c))
        for hh in range(2):
            send_c(below[hh], (other, c))
            send_c(above[hh], (other, c))

    def c_far():
        for hh in range(2):
            wait_c(beyond[hh])
            send_c(beyond[hh], (other, c))

    def c_across(d):
        for t in across[2 * d : 2 * d + 2]:
            wait_c(t)

    def r_end():
        for t in opposite:
            wait_r(t)

    def bring(piece):
        base, wide = PIECES[piece]
        p, w = base // 128, wide // 128
        s_old = jnp.concatenate([ss[t, 0:base] for t in range(16)], 1)
        s_new = jnp.concatenate([ss[t, base : base + wide] for t in range(16)], 1)
        g_new = dot_nt(s_new, s_new)
        i = lax.broadcasted_iota(jnp.int32, (wide, wide), 0)
        j = lax.broadcasted_iota(jnp.int32, (wide, wide), 1)
        m_new = jnp.where(i == j, g_new + ridge_value, alpha_scale * g_new)
        one = jnp.where(i == j, 1.0, 0.0)
        if base:
            g_mix = alpha_scale * dot_nt(s_old, s_new)
            w_old = jnp.concatenate([m4[0 : 16 * p, 4 + t].reshape(base, 128) for t in range(p)], 1)
            wh, wm, wl = split3(w_old)
            u = jnp.dot(
                jnp.concatenate([wh, wh, wh, wm, wm, wl], 1), six_right(g_mix), preferred_element_type=F32
            )
            below_it = dot_tn(six_left(u), six_right(jnp.concatenate([u, w_old], 1)))
            m_new = m_new - below_it[:, :wide]
        rows = slice(16 * p, 16 * (p + w))
        for t in range(w):
            cut = slice(128 * t, 128 * t + 128)
            if base:
                m4[0 : 16 * p, p + t] = u[:, cut].reshape(16 * p, 8, 128)
            m4[rows, p + t] = m_new[:, cut].reshape(16 * w, 8, 128)
            m4[rows, 4 + p + t] = one[:, cut].reshape(16 * w, 8, 128)
        for t in range(p):
            m4[rows, 4 + t] = (-below_it[:, wide + 128 * t : wide + 128 * t + 128]).reshape(16 * w, 8, 128)

    s_x(0)
    copy(cs.at[r], rs.at[r], rrecv.at[r], (goes_row, goes_col), moves)
    s_x(1)
    s_x(2)
    s_z(0)
    s_z(1)
    s_z(2)
    s_y(0)
    r_first()
    s_core(0)
    s_y(1)
    s_end(0)

    hooks = [
        (0, lambda: bring(0)),
        (0, lambda: s_y(2)),
        (1, c_first),
        (2, lambda: r_line(1)),
        (3, lambda: s_core(1)),
        (5, lambda: r_ring(0)),
        (7, lambda: r_line(2)),
        (7, lambda: s_core(2)),
        (8, lambda: s_end(1)),
        (8, lambda: bring(1)),
        (10, lambda: r_ring(1)),
        (12, lambda: r_line(3)),
        (13, c_twin),
        (16, lambda: r_ring(2)),
        (16, lambda: s_end(2)),
        (16, lambda: bring(2)),
        (19, c_pass),
        (20, lambda: r_ring(3)),
        (17, lambda: c_across(0)),
        (22, lambda: c_across(1)),
        (23, lambda: c_across(3)),
        (26, c_far),
        (28, lambda: c_across(2)),
        (30, r_end),
    ]

    m4[...] = jnp.zeros_like(m4)

    def group(slab, total, task_row, start):
        tasks = [4 * task_row + q for q in range(4)]
        add = dot_nt(
            jnp.concatenate([slab[t] for t in tasks], 1), jnp.concatenate([ss[t] for t in tasks], 1)
        )
        total[...] = add if start else total[...] + add

    group_own, group_left, group_right, group_far = [(2 * y - xx + 8) % 4 for xx in (x, x - 1, x + 1, x + 2)]
    y_down, y_up, y_far = (y + 3) % 4, (y + 1) % 4, (y + 2) % 4
    beside = [
        (17, lambda: group(rs, yr, group_own, True)),
        (18, lambda: group(cs, yc, y, True)),
        (21, lambda: group(rs, yr, group_left, False)),
        (22, lambda: group(rs, yr, group_right, False)),
        (23, lambda: group(cs, yc, y_down, False)),
        (24, lambda: group(cs, yc, y_up, False)),
        (29, lambda: group(cs, yc, y_far, False)),
        (31, lambda: group(rs, yr, group_far, False)),
    ]
    factor(m4, hooks, beside)

    wide = [jnp.concatenate([m4[pl.ds(16 * b, 16), 4 + t].reshape(128, 128) for b in range(4)], 0) for t in range(4)]
    w_high, w_low = two(jnp.concatenate(wide, 1))

    def solve(y_ref):
        y_high, y_low = two(alpha_scale * y_ref[...])
        parts = []
        for n in (256, 512):
            yh, yl = y_high[:, :n], y_low[:, :n]
            wh, wl = w_high[n - 256 : n, :n], w_low[n - 256 : n, :n]
            parts.append(
                two(dot_nt(jnp.concatenate([yh, yh, yl], 1), jnp.concatenate([wh, wl, wh], 1)))
            )
        return [jnp.concatenate([p[q] for p in parts], 1) for q in range(2)]

    pc_high, pc_low = solve(yc)
    pc[...] = jnp.concatenate([pc_high, pc_low, pc_high], 1)
    pr_high, pr_low = solve(yr)
    pr[...] = jnp.concatenate([pr_high, pr_high, pr_low], 1)
    c_all = jnp.concatenate([cs[t] for t in range(16)], 1)
    r_all = jnp.concatenate([rs[t] for t in range(16)], 1)

    w_mine = jnp.concatenate([m4[pl.ds(4 * c, 4), 4 + t].reshape(32, 128) for t in range(4)], 1)
    wm_high, wm_low = two(w_mine)
    y_high, y_low = two(alpha_scale * yr[...])
    panels[...] = dot_nt(
        jnp.concatenate([wm_high, wm_low, wm_high], 1), jnp.concatenate([y_high, y_high, y_low], 1)
    )

    @pl.when(r == 0)
    def _():
        i = lax.broadcasted_iota(jnp.int32, (32, 128), 0) + 32 * c
        for t in range(4):
            u = m4[pl.ds(4 * c, 4), t].reshape(32, 128)
            j = lax.broadcasted_iota(jnp.int32, (32, 128), 1) + 128 * t
            panels[:, 128 * t : 128 * t + 128] = jnp.where(j >= i, u, 0.0)

    p_left, p_right = pr[...], pc[...]
    row0 = jnp.where(r == 0, 512, 0)
    col0 = jnp.where(c == 0, 512, 0)
    for n in range(0, 800, 256):
        w = min(256, 800 - n)
        g = dot_nt(r_all, c_all[n : n + w])
        pp = dot_nt(p_left, p_right[n : n + w])
        i = lax.broadcasted_iota(jnp.int32, (800, w), 0)
        j = lax.broadcasted_iota(jnp.int32, (800, w), 1) + n
        m = jnp.where(i == jnp.where(r == c, j, -1), g + ridge_value, alpha_scale * g) - pp
        trailing[:, n : n + w] = jnp.where(jnp.logical_and(i >= row0, j >= col0), m, 0.0)

    for at, (cond, src) in enumerate(pending):
        sent = pltpu.make_async_remote_copy(
            src_ref=src, dst_ref=src, send_sem=send.at[at], recv_sem=crecv.at[0], device_id=(other, c), device_id_type=MESH
        ).wait_send
        if cond is None:
            sent()
        else:
            pl.when(cond)(sent)


def body(activations, task_weight):
    vmem = pl.BlockSpec(memory_space=pltpu.VMEM)
    trailing, panels = pl.pallas_call(
        kernel,
        out_shape=(
            jax.ShapeDtypeStruct((800, 800), F32),
            jax.ShapeDtypeStruct((32, 800), F32),
        ),
        in_specs=[vmem, pl.BlockSpec(memory_space=pltpu.SMEM)],
        out_specs=(vmem, vmem),
        scratch_shapes=[
            pltpu.VMEM((16, 800, 128), BF),
            pltpu.VMEM((16, 800, 128), BF),
            pltpu.VMEM((16, 512, 128), BF),
            pltpu.VMEM((64, 8, 8, 128), F32),
            pltpu.VMEM((800, 512), F32),
            pltpu.VMEM((800, 512), F32),
            pltpu.VMEM((800, 1536), BF),
            pltpu.VMEM((800, 1536), BF),
            pltpu.SemaphoreType.DMA((128,)),
            pltpu.SemaphoreType.DMA((16,)),
            pltpu.SemaphoreType.DMA((16,)),
            pltpu.SemaphoreType.DMA((16, 3)),
        ],
        compiler_params=pltpu.CompilerParams(
            collective_id=0, has_side_effects=True, vmem_limit_bytes=60 << 20
        ),
    )(activations.T, task_weight)
    return trailing, panels.T


def solution(mesh):
    placed = (P("row", "col"), P())
    return jax.shard_map(
        body,
        mesh=mesh,
        in_specs=placed,
        out_specs=(P("row", "col"), P("row", "col")),
        check_vma=False,
    )
```

```python
import jax
import jax.numpy as jnp
from jax import lax
from jax.experimental import pallas as pl
from jax.experimental.pallas import tpu as pltpu
from jax.sharding import PartitionSpec as P

TOK = 128
PANEL = 256
LEAF = 16
PIECES = ((0, 128), (128, 128), (256, 256))

alpha_scale = 0.9
ridge_value = 0.2

F32 = jnp.float32
BF = jnp.bfloat16
MESH = pl.DeviceIdType.MESH


def dot_nt(a, b):
    return lax.dot_general(a, b, (((1,), (1,)), ((), ())), preferred_element_type=F32)


def dot_tn(a, b):
    return lax.dot_general(a, b, (((0,), (0,)), ((), ())), preferred_element_type=F32)


def split3(x):
    high = x.astype(BF)
    rest = x - high.astype(F32)
    mid = rest.astype(BF)
    low = (rest - mid.astype(F32)).astype(BF)
    return high, mid, low


def six_left(x):
    h, m, l = split3(x)
    return jnp.concatenate([h, h, h, m, m, l], 0)


def six_right(x):
    h, m, l = split3(x)
    return jnp.concatenate([h, m, l, h, m, h], 0)


def two(x):
    high = x.astype(BF)
    return high, (x - high.astype(F32)).astype(BF)


def sub_cast(x, s):
    return jnp.broadcast_to(x[s : s + 1, :], (8, 128))


def lane_cast(x, k):
    return jnp.broadcast_to(x[:, k : k + 1], (8, 128))


def chain8(s, rows, cols):
    for k in range(8):
        r = lax.rsqrt(s[k, k])
        for j in range(k + 1, 8):
            s[j, k] = s[j, k] * r
        for q in range(k + 1, 8):
            for j in range(q, 8):
                s[j, q] = s[j, q] - s[j, k] * s[q, k]
        rows[k] = rows[k] * r
        for j in range(k + 1, 8):
            rows[j] = rows[j] - s[j, k] * rows[k]
        if cols is not None:
            cols[k] = cols[k] * r
            for q in range(k + 1, 8):
                cols[q] = cols[q] - cols[k] * s[q, k]


def leaf_factor(m4, kb, leaf):
    i0 = kb * 16 + 2 * leaf
    o = LEAF * leaf
    d0 = m4[i0, kb]
    d1 = m4[i0 + 1, kb]
    s = {}
    for k in range(8):
        column = lane_cast(d0, o + k)
        for j in range(k, 8):
            s[j, k] = sub_cast(column, j)
    cols = [lane_cast(d1, o + k) for k in range(16)]
    upper = [m4[i0, :, q, :] for q in range(8)]
    first = cols[:8]
    chain8(s, upper, first)
    for q in range(8):
        m4[i0, :, q, :] = upper[q]
    lower = [m4[i0 + 1, :, q, :] for q in range(8)]
    second = cols[8:]
    for k in range(8):
        t = [sub_cast(first[k], q) for q in range(8)]
        for q in range(8):
            second[q] = second[q] - first[k] * t[q]
        for q in range(8):
            lower[q] = lower[q] - t[q] * upper[k]
    s = {}
    for k in range(8):
        for j in range(k, 8):
            s[j, k] = sub_cast(second[k], j)
    chain8(s, lower, None)
    for q in range(8):
        m4[i0 + 1, :, q, :] = lower[q]


def inner_update(m4, kb, leaf):
    i0 = kb * 16 + 2 * leaf
    u = m4[pl.ds(i0, 2), pl.ds(kb, 5)]
    tiles = [u[:, t].reshape(16, 128) for t in range(5)]
    left = six_left(tiles[0])[:, LEAF * (leaf + 1) :]
    up = dot_tn(left, six_right(jnp.concatenate(tiles, 1)))
    for q in range((7 - leaf) * 2):
        for t in range(5):
            m4[i0 + 2 + q, kb + t] = (
                m4[i0 + 2 + q, kb + t] - up[8 * q : 8 * q + 8, 128 * t : 128 * t + 128]
            )


def rest_update(m4, kb, b):
    left = six_left(m4[pl.ds(kb * 16, 16), b].reshape(128, 128))
    for half in range(2):
        w = jnp.concatenate(
            [m4[pl.ds(kb * 16, 16), kb + 1 + 2 * half + t].reshape(128, 128) for t in range(2)], 1
        )
        up = dot_tn(left, six_right(w))
        for t in range(2):
            tt = kb + 1 + 2 * half + t
            m4[pl.ds(b * 16, 16), tt] = m4[pl.ds(b * 16, 16), tt] - up[
                :, 128 * t : 128 * t + 128
            ].reshape(16, 8, 128)


def factor(m4, hooks, beside):
    def early(kb, _):
        for leaf in range(8):
            for at, run in hooks:
                if at < 16 and at % 8 == leaf:
                    pl.when(kb == at // 8)(run)
            leaf_factor(m4, kb, leaf)
            if leaf < 7:
                inner_update(m4, kb, leaf)
        return 0

    lax.fori_loop(0, 2, early, 0)
    for kb in (2, 3):
        for leaf in range(8):
            for at, run in hooks:
                if at == 8 * kb + leaf:
                    run()
            for at, run in beside:
                if at == 8 * kb + leaf:
                    run()
            leaf_factor(m4, kb, leaf)
            if leaf < 7:
                inner_update(m4, kb, leaf)
        if kb == 2:
            rest_update(m4, 2, 3)


def kernel(act, weight, trailing, panels, cs, rs, ss, m4, yr, yc, pr, pc, send, crecv, rrecv, srecv):
    r = lax.axis_index("row")
    c = lax.axis_index("col")
    y, h, k = r // 4, (r // 2) % 2, r % 2
    x, l = c // 4, c % 4

    def row_at(yy, hh, kk):
        return 4 * ((yy + 4) % 4) + 2 * hh + kk

    def col_at(xx, ll):
        return 4 * ((xx + 8) % 4) + ll

    def slot_at(xx, ll):
        return 4 * ((2 * y - xx + 8) % 4) + 2 * ((ll // 2 + k + h) % 2) + ll % 2

    mine = slot_at(x, l)
    goes_row = c
    goes_col = col_at(2 * x - y, 2 * ((h + l // 2 + l % 2) % 2) + k)
    moves = jnp.logical_or(goes_row != r, goes_col != c)
    stays = jnp.logical_not(moves)

    zring = [(r, col_at(x, (l + d) % 4)) for d in (1, 2, 3)]
    zring += [(row_at(y, 1 - h, k), col_at(x, (l + d) % 4)) for d in (0, 1, 2, 3)]
    partners = zring + [
        (r, col_at(x + 1, l)),
        (r, col_at(x - 1, l)),
        (row_at(y + 1, h, k), c),
        (row_at(y - 1, h, k), c),
        (row_at(y, h, 1 - k), c),
        (r, col_at(x + 2, l)),
        (row_at(y + 2, h, k), c),
    ]
    barrier = pltpu.get_barrier_semaphore()
    for p in partners:
        pl.semaphore_signal(barrier, inc=1, device_id=p, device_id_type=MESH)

    @pl.when(moves)
    def _():
        pl.semaphore_signal(barrier, inc=1, device_id=(mine, r), device_id_type=MESH)

    scale = jnp.sqrt(jnp.full((8, 128), weight[r], F32) / TOK)[0:1, 0:1]
    cs[r] = (act[...].astype(F32) * scale).astype(BF)

    @pl.when(c == 0)
    def _():
        ss[r] = cs[r, 0:512]

    @pl.when(stays)
    def _():
        rs[r] = cs[r]

    pl.semaphore_wait(barrier, jnp.where(stays, len(partners), len(partners) + 1))

    pending = []

    def copy(src, dst, recv, target, cond=None):
        d = pltpu.make_async_remote_copy(
            src_ref=src,
            dst_ref=dst,
            send_sem=send.at[len(pending)],
            recv_sem=recv,
            device_id=target,
            device_id_type=MESH,
        )
        if cond is None:
            d.start()
        else:
            pl.when(cond)(d.start)
        pending.append((cond, src))

    def send_c(t, target):
        copy(cs.at[t], cs.at[t], crecv.at[t], target)

    def send_r(t, target):
        copy(rs.at[t], rs.at[t], rrecv.at[t], target)

    def s_ref(t, half):
        return ss.at[t, pl.ds(*PIECES[half])]

    def send_s(t, half, target, cond=None):
        copy(s_ref(t, half), s_ref(t, half), srecv.at[t, half], target, cond)

    def arrived(ref, sem):
        pltpu.make_async_remote_copy(
            src_ref=ref, dst_ref=ref, send_sem=send.at[0], recv_sem=sem, device_id=(r, c), device_id_type=MESH
        ).wait_recv()

    def wait_c(t):
        arrived(cs.at[t], crecv.at[t])

    def wait_r(t):
        arrived(rs.at[t], rrecv.at[t])

    def wait_s(t, half):
        arrived(s_ref(t, half), srecv.at[t, half])

    twin = row_at(y, 1 - h, k)
    up, down = row_at(y + 1, h, k), row_at(y - 1, h, k)
    right, left = col_at(x + 1, l), col_at(x - 1, l)
    other = row_at(y, h, 1 - k)

    down_line = [jnp.maximum(l - d, 0) for d in range(4)]
    up_line = [jnp.minimum(l + d, 3) for d in range(4)]
    minus = [slot_at(x, ll) for ll in down_line]
    plus = [slot_at(x, ll) for ll in up_line]
    minus_on_left = [slot_at(x - 1, ll) for ll in down_line]
    minus_on_right = [slot_at(x + 1, ll) for ll in down_line]
    plus_on_left = [slot_at(x - 1, ll) for ll in up_line]
    plus_on_right = [slot_at(x + 1, ll) for ll in up_line]
    from_minus = [l >= d for d in range(4)]
    from_plus = [l + d <= 3 for d in range(4)]
    pass_plus = [jnp.logical_and(l >= d, l <= 2) for d in range(4)]
    pass_minus = [jnp.logical_and(l + d <= 3, l >= 1) for d in range(4)]
    odd_slot = [(c + d) % 2 == 1 for d in range(4)]
    even_slot = [(c + d) % 2 == 0 for d in range(4)]
    side = [
        [jnp.logical_and(v, p) for v, p in zip(f, par)]
        for f in (from_minus, from_plus)
        for par in (even_slot, odd_slot)
    ]
    before, after = 4 * x + down_line[1], 4 * x + up_line[1]
    below = [row_at(y - 1, hh, k) for hh in range(2)]
    above = [row_at(y + 1, hh, k) for hh in range(2)]
    beyond = [row_at(y + 2, hh, k) for hh in range(2)]
    across = [row_at(y + d, hh, 1 - k) for d in range(4) for hh in range(2)]
    own_two = (r, twin)
    opposite = [slot_at(x + 2, ll) for ll in range(4)]
    far_row, far_col = row_at(y + 2, h, k), col_at(x + 2, l)

    at_l0 = l == 0
    off_l0 = l != 0
    source = c == 0
    passes_z = jnp.logical_and(at_l0, x != 0)

    def s_x(half):
        for target in (right, left, far_col):
            send_s(r, half, (r, target), source)

    def s_z(half):
        pl.when(passes_z)(lambda: wait_s(r, half))
        for p in zring:
            send_s(r, half, p, at_l0)

    def s_y(half):
        pl.when(off_l0)(lambda: wait_s(r, half))
        wait_s(twin, half)
        for t in own_two:
            send_s(t, half, (up, c))
            send_s(t, half, (down, c))
            send_s(t, half, (far_row, c))
        for t in own_two:
            send_s(t, half, (other, c))

    def s_core(half):
        for group in (below, above, beyond):
            for t in group:
                wait_s(t, half)
                send_s(t, half, (other, c))

    def s_end(half):
        for t in across:
            wait_s(t, half)

    def r_first():
        pl.when(moves)(lambda: wait_r(mine))
        copy(rs.at[mine], rs.at[mine], rrecv.at[mine], (r, after), pass_plus[0])
        copy(rs.at[mine], rs.at[mine], rrecv.at[mine], (r, before), pass_minus[0])
        send_r(mine, (r, right))
        send_r(mine, (r, left))

    def r_line(d):
        def from_before():
            wait_r(minus[d])

        def from_after():
            wait_r(plus[d])

        pl.when(from_minus[d])(from_before)
        pl.when(from_plus[d])(from_after)
        copy(rs.at[minus[d]], rs.at[minus[d]], rrecv.at[minus[d]], (r, after), pass_plus[d])
        copy(rs.at[plus[d]], rs.at[plus[d]], rrecv.at[plus[d]], (r, before), pass_minus[d])
        for target in (right, left):
            copy(rs.at[minus[d]], rs.at[minus[d]], rrecv.at[minus[d]], (r, target), from_minus[d])
            copy(rs.at[plus[d]], rs.at[plus[d]], rrecv.at[plus[d]], (r, target), from_plus[d])

    def r_ring(d):
        ways = [(from_minus, minus_on_left, minus_on_right, 0)]
        if d > 0:
            ways.append((from_plus, plus_on_left, plus_on_right, 2))
        for there, on_left, on_right, at in ways:

            def both():
                wait_r(on_left[d])
                wait_r(on_right[d])

            pl.when(there[d])(both)
            copy(rs.at[on_left[d]], rs.at[on_left[d]], rrecv.at[on_left[d]], (r, right), side[at][d])
            copy(rs.at[on_right[d]], rs.at[on_right[d]], rrecv.at[on_right[d]], (r, left), side[at + 1][d])

    def c_first():
        send_c(r, (twin, c))
        send_c(r, (up, c))
        send_c(r, (down, c))
        send_c(r, (other, c))

    def c_twin():
        wait_c(twin)
        send_c(twin, (up, c))
        send_c(twin, (down, c))
        send_c(twin, (other, c))

    def c_pass():
        for hh in range(2):
            wait_c(below[hh])
            wait_c(above[hh])
        send_c(below[0], (up, c))
        send_c(above[1], (down, c))
        for hh in range(2):
            send_c(below[hh], (other, c))
            send_c(above[hh], (other, c))

    def c_far():
        for hh in range(2):
            wait_c(beyond[hh])
            send_c(beyond[hh], (other, c))

    def c_across(d):
        for t in across[2 * d : 2 * d + 2]:
            wait_c(t)

    def r_end():
        for t in opposite:
            wait_r(t)

    def bring(piece):
        base, wide = PIECES[piece]
        p, w = base // 128, wide // 128
        s_old = jnp.concatenate([ss[t, 0:base] for t in range(16)], 1)
        s_new = jnp.concatenate([ss[t, base : base + wide] for t in range(16)], 1)
        g_new = dot_nt(s_new, s_new)
        i = lax.broadcasted_iota(jnp.int32, (wide, wide), 0)
        j = lax.broadcasted_iota(jnp.int32, (wide, wide), 1)
        m_new = jnp.where(i == j, g_new + ridge_value, alpha_scale * g_new)
        one = jnp.where(i == j, 1.0, 0.0)
        if base:
            g_mix = alpha_scale * dot_nt(s_old, s_new)
            w_old = jnp.concatenate([m4[0 : 16 * p, 4 + t].reshape(base, 128) for t in range(p)], 1)
            wh, wm, wl = split3(w_old)
            u = jnp.dot(
                jnp.concatenate([wh, wh, wh, wm, wm, wl], 1), six_right(g_mix), preferred_element_type=F32
            )
            below_it = dot_tn(six_left(u), six_right(jnp.concatenate([u, w_old], 1)))
            m_new = m_new - below_it[:, :wide]
        rows = slice(16 * p, 16 * (p + w))
        for t in range(w):
            cut = slice(128 * t, 128 * t + 128)
            if base:
                m4[0 : 16 * p, p + t] = u[:, cut].reshape(16 * p, 8, 128)
            m4[rows, p + t] = m_new[:, cut].reshape(16 * w, 8, 128)
            m4[rows, 4 + p + t] = one[:, cut].reshape(16 * w, 8, 128)
        for t in range(p):
            m4[rows, 4 + t] = (-below_it[:, wide + 128 * t : wide + 128 * t + 128]).reshape(16 * w, 8, 128)

    s_x(0)
    copy(cs.at[r], rs.at[r], rrecv.at[r], (goes_row, goes_col), moves)
    s_x(1)
    s_x(2)
    s_z(0)
    s_z(1)
    s_z(2)
    s_y(0)
    r_first()
    s_core(0)
    s_y(1)
    s_end(0)

    hooks = [
        (0, lambda: bring(0)),
        (0, lambda: s_y(2)),
        (1, c_first),
        (3, lambda: r_line(1)),
        (3, lambda: s_core(1)),
        (6, lambda: r_ring(0)),
        (8, lambda: r_line(2)),
        (7, lambda: s_core(2)),
        (8, lambda: s_end(1)),
        (8, lambda: bring(1)),
        (11, lambda: r_ring(1)),
        (13, lambda: r_line(3)),
        (14, c_twin),
        (17, lambda: r_ring(2)),
        (16, lambda: s_end(2)),
        (16, lambda: bring(2)),
        (20, c_pass),
        (20, lambda: r_ring(3)),
        (17, lambda: c_across(0)),
        (22, lambda: c_across(1)),
        (23, lambda: c_across(3)),
        (26, c_far),
        (28, lambda: c_across(2)),
        (30, r_end),
    ]

    m4[...] = jnp.zeros_like(m4)

    def group(slab, total, task_row, start):
        tasks = [4 * task_row + q for q in range(4)]
        add = dot_nt(
            jnp.concatenate([slab[t] for t in tasks], 1), jnp.concatenate([ss[t] for t in tasks], 1)
        )
        total[...] = add if start else total[...] + add

    group_own, group_left, group_right, group_far = [(2 * y - xx + 8) % 4 for xx in (x, x - 1, x + 1, x + 2)]
    y_down, y_up, y_far = (y + 3) % 4, (y + 1) % 4, (y + 2) % 4
    def early_columns():
        first_w = jnp.concatenate([m4[0:32, 4 + t].reshape(256, 128) for t in range(2)], 1)
        wh, wl = two(first_w)
        yh, yl = two(alpha_scale * yc[:, 0:256])
        high, low = two(dot_nt(jnp.concatenate([yh, yh, yl], 1), jnp.concatenate([wh, wl, wh], 1)))
        pc[:, 0:256] = high
        pc[:, 512:768] = low
        pc[:, 1024:1280] = high

    beside = [
        (17, lambda: group(rs, yr, group_own, True)),
        (18, lambda: group(cs, yc, y, True)),
        (21, lambda: group(rs, yr, group_left, False)),
        (22, lambda: group(rs, yr, group_right, False)),
        (23, lambda: group(cs, yc, y_down, False)),
        (24, lambda: group(cs, yc, y_up, False)),
        (29, lambda: group(cs, yc, y_far, False)),
        (30, early_columns),
        (31, lambda: group(rs, yr, group_far, False)),
    ]
    factor(m4, hooks, beside)

    wide = [jnp.concatenate([m4[pl.ds(16 * b, 16), 4 + t].reshape(128, 128) for b in range(4)], 0) for t in range(4)]
    w_high, w_low = two(jnp.concatenate(wide, 1))

    def solve(y_ref, widths):
        y_high, y_low = two(alpha_scale * y_ref[...])
        parts = []
        for n in widths:
            yh, yl = y_high[:, :n], y_low[:, :n]
            wh, wl = w_high[n - 256 : n, :n], w_low[n - 256 : n, :n]
            parts.append(
                two(dot_nt(jnp.concatenate([yh, yh, yl], 1), jnp.concatenate([wh, wl, wh], 1)))
            )
        return [jnp.concatenate([p[q] for p in parts], 1) for q in range(2)]

    pc_high, pc_low = solve(yc, (512,))
    pc[:, 256:512] = pc_high
    pc[:, 768:1024] = pc_low
    pc[:, 1280:1536] = pc_high
    pr_high, pr_low = solve(yr, (256, 512))
    pr[...] = jnp.concatenate([pr_high, pr_high, pr_low], 1)
    c_all = jnp.concatenate([cs[t] for t in range(16)], 1)
    r_all = jnp.concatenate([rs[t] for t in range(16)], 1)

    w_mine = jnp.concatenate([m4[pl.ds(4 * c, 4), 4 + t].reshape(32, 128) for t in range(4)], 1)
    wm_high, wm_low = two(w_mine)
    y_high, y_low = two(alpha_scale * yr[...])
    panels[...] = dot_nt(
        jnp.concatenate([wm_high, wm_low, wm_high], 1), jnp.concatenate([y_high, y_high, y_low], 1)
    )

    @pl.when(r == 0)
    def _():
        i = lax.broadcasted_iota(jnp.int32, (32, 128), 0) + 32 * c
        for t in range(4):
            u = m4[pl.ds(4 * c, 4), t].reshape(32, 128)
            j = lax.broadcasted_iota(jnp.int32, (32, 128), 1) + 128 * t
            panels[:, 128 * t : 128 * t + 128] = jnp.where(j >= i, u, 0.0)

    p_left, p_right = pr[...], pc[...]
    row0 = jnp.where(r == 0, 512, 0)
    col0 = jnp.where(c == 0, 512, 0)
    for n in range(0, 800, 256):
        w = min(256, 800 - n)
        g = dot_nt(r_all, c_all[n : n + w])
        pp = dot_nt(p_left, p_right[n : n + w])
        i = lax.broadcasted_iota(jnp.int32, (800, w), 0)
        j = lax.broadcasted_iota(jnp.int32, (800, w), 1) + n
        m = jnp.where(i == jnp.where(r == c, j, -1), g + ridge_value, alpha_scale * g) - pp
        trailing[:, n : n + w] = jnp.where(jnp.logical_and(i >= row0, j >= col0), m, 0.0)

    for at, (cond, src) in enumerate(pending):
        sent = pltpu.make_async_remote_copy(
            src_ref=src, dst_ref=src, send_sem=send.at[at], recv_sem=crecv.at[0], device_id=(other, c), device_id_type=MESH
        ).wait_send
        if cond is None:
            sent()
        else:
            pl.when(cond)(sent)


def body(activations, task_weight):
    vmem = pl.BlockSpec(memory_space=pltpu.VMEM)
    trailing, panels = pl.pallas_call(
        kernel,
        out_shape=(
            jax.ShapeDtypeStruct((800, 800), F32),
            jax.ShapeDtypeStruct((32, 800), F32),
        ),
        in_specs=[vmem, pl.BlockSpec(memory_space=pltpu.SMEM)],
        out_specs=(vmem, vmem),
        scratch_shapes=[
            pltpu.VMEM((16, 800, 128), BF),
            pltpu.VMEM((16, 800, 128), BF),
            pltpu.VMEM((16, 512, 128), BF),
            pltpu.VMEM((64, 8, 8, 128), F32),
            pltpu.VMEM((800, 512), F32),
            pltpu.VMEM((800, 512), F32),
            pltpu.VMEM((800, 1536), BF),
            pltpu.VMEM((800, 1536), BF),
            pltpu.SemaphoreType.DMA((128,)),
            pltpu.SemaphoreType.DMA((16,)),
            pltpu.SemaphoreType.DMA((16,)),
            pltpu.SemaphoreType.DMA((16, 3)),
        ],
        compiler_params=pltpu.CompilerParams(
            collective_id=0, has_side_effects=True, vmem_limit_bytes=60 << 20
        ),
    )(activations.T, task_weight)
    return trailing, panels.T


def solution(mesh):
    placed = (P("row", "col"), P())
    return jax.shard_map(
        body,
        mesh=mesh,
        in_specs=placed,
        out_specs=(P("row", "col"), P("row", "col")),
        check_vma=False,
    )
```
